512 devices in a mesh: band: 32 (over z, core), fft: 16 (over y, x).
Axes of the slice: x: 4, y: 4, z: 16, core: 2. Of those that a mesh axis runs over, the one named last changes fastest.
Arguments:
- orbitals: bfloat16 [32, 128, 128, 128], P('band', 'fft'), may hold values from -6 to 6
- kernel: float32 [128, 128, 128], P(None, 'fft'), may hold values from 0.05 to 1
Outputs:
- exchange: float32 [32, 128, 128, 128], P('band', 'fft')
The draws below stay inside these ranges and needn't reach their ends.
All inputs are finite; a program needn't handle non-finite values.
Results may differ from the reference program's by a relative error of at most 0.0095.
Values may be sent and summed in bfloat16 or wider, within the bound.
No kernel may reach another device: no remote copies, remote signals or barrier semaphores. Data moves between devices by JAX's collectives and lax.ppermute only.
A program may use at most 64 MiB of HBM per device.

```python
import math
import jax
import jax.numpy as jnp
import numpy as np
from jax import lax

NG = 128
BB = 1
NB = 32


def block_levels(key, shape, pieces, low, high):
    def one(position, shards_of):
        draws = jax.random.uniform(jax.random.fold_in(jax.random.fold_in(key, 6), position), (shards_of,), jnp.float32, low / len(pieces), high / len(pieces))
        return jnp.repeat(jnp.exp(draws), shape[position] // shards_of).reshape((-1,) + (1,) * (len(shape) - position - 1))

    gain = one(*pieces[0])
    for cut in pieces[1:]:
        gain = gain * one(*cut)
    return gain


def bell_draw(key, dims, spread, limit, cuts=(), held_as=jnp.bfloat16):
    factor_of = block_levels(key, dims, cuts, -0.22, 0.18) if cuts else 1.0
    drawn = jax.random.normal(key, dims, jnp.float32) * spread * factor_of
    return jnp.minimum(jnp.maximum(drawn, -limit), limit).astype(held_as)


def setup_inputs(seed: int = 0) -> dict:
    keys = jax.random.split(jax.random.key(seed), 3)
    return {
        "orbitals": bell_draw(keys[0], (NB, NG, NG, NG), 1.0, 6.0, ((0, 32), (1, 16))),
        "kernel": jnp.clip(jnp.exp(math.log(1.0) - 2.9957323 * jax.random.uniform(keys[1], (NG, NG, NG), jnp.float32) ** block_levels(keys[1], (NG, NG, NG), ((1, 16),), -0.2, 0.2)), 0.05, 1.0),
    }


def make_tables():
    index = jnp.arange(NG, dtype=jnp.int32)
    phase = index[:, None] * index[None, :] % NG
    angle = phase.astype(jnp.float32) * (2.0 * math.pi / NG)
    factor = 1.0 / math.sqrt(NG)
    return ((jnp.cos(angle) * factor).astype(jnp.bfloat16), (jnp.sin(angle) * factor).astype(jnp.bfloat16))

def contract(spec, field, table):
    return jnp.einsum(spec, field.astype(jnp.float32), table.astype(jnp.float32))

def section(real_part, imag_part, cosm, sinm, spec, sign):
    out_real = contract(spec, real_part, cosm) - sign * contract(spec, imag_part, sinm)
    out_imag = contract(spec, imag_part, cosm) + sign * contract(spec, real_part, sinm)
    return (out_real.astype(jnp.bfloat16), out_imag.astype(jnp.bfloat16))

def pair_lists(count):
    first, second, mirrored = ([], [], [])
    for i in range(count):
        for j in range(i, count):
            first.append(i)
            second.append(j)
            mirrored.append(j != i)
    for i in range(count):
        for j in range(count):
            first.append(i)
            second.append(count + j)
            mirrored.append(True)
    return (first, second, mirrored)

def block_terms(both, kernel, cosm, sinm):
    first, second, mirrored = pair_lists(BB)
    left_rows = both[np.array(first)]
    right_rows = both[np.array(second)]
    density = (left_rows.astype(jnp.float32) * right_rows.astype(jnp.float32)).astype(jnp.bfloat16)
    real_part = contract('pxyz,zk->pxyk', density, cosm).astype(jnp.bfloat16)
    imag_part = (-contract('pxyz,zk->pxyk', density, sinm)).astype(jnp.bfloat16)
    real_part, imag_part = section(real_part, imag_part, cosm, sinm, 'pxyz,yk->pxkz', -1.0)
    real_part, imag_part = section(real_part, imag_part, cosm, sinm, 'pxyz,xk->pkyz', -1.0)
    real_part = (real_part.astype(jnp.float32) * kernel).astype(jnp.bfloat16)
    imag_part = (imag_part.astype(jnp.float32) * kernel).astype(jnp.bfloat16)
    real_part, imag_part = section(real_part, imag_part, cosm, sinm, 'pxyz,xk->pkyz', 1.0)
    real_part, imag_part = section(real_part, imag_part, cosm, sinm, 'pxyz,yk->pxkz', 1.0)
    potential = (contract('pxyz,zk->pxyk', real_part, cosm) - contract('pxyz,zk->pxyk', imag_part, sinm)).astype(jnp.bfloat16)
    potential = potential.astype(jnp.float32)
    totals = [jnp.zeros(both.shape[1:], jnp.float32) for target in range(2 * BB)]
    for pair in range(len(first)):
        totals[first[pair]] = totals[first[pair]] + potential[pair] * right_rows[pair].astype(jnp.float32)
        if mirrored[pair]:
            totals[second[pair]] = totals[second[pair]] + potential[pair] * left_rows[pair].astype(jnp.float32)
    return (jnp.stack(totals[:BB]), jnp.stack(totals[BB:]))

def reference(orbitals, kernel):
    cosm, sinm = make_tables()
    blocks = NB // BB

    def one_block(block):
        start = (block * BB).astype(jnp.int32)
        after = ((block + 1) % blocks * BB).astype(jnp.int32)
        own_rows = lax.dynamic_slice_in_dim(orbitals, start, BB, 0)
        next_rows = lax.dynamic_slice_in_dim(orbitals, after, BB, 0)
        both = jnp.concatenate([own_rows, next_rows], axis=0)
        return block_terms(both, kernel, cosm, sinm)
    own_terms, next_terms = lax.map(one_block, jnp.arange(blocks, dtype=jnp.int32))
    moved = jnp.roll(next_terms, 1, axis=0)
    total = own_terms + moved
    return total.reshape((NB,) + orbitals.shape[1:])
```

```python
import math

import jax
import jax.numpy as jnp
import numpy as np
from jax import lax
from jax.experimental import pallas as pl
from jax.experimental.pallas import tpu as pltpu
from jax.sharding import PartitionSpec as P

F32 = jnp.float32
BF16 = jnp.bfloat16
VMEM_LIMIT = 16 * 1024 * 1024


def from_behind(shard, axis, by):
    devices = lax.axis_size(axis)
    return lax.ppermute(shard, axis, [(i, (i + by) % devices) for i in range(devices)])


def make_tables(length):
    index = np.arange(length)
    angle = (index[:, None] * index[None, :] % length).astype(np.float32)
    angle = angle * np.float32(2.0 * math.pi / length)
    factor = np.float32(1.0 / math.sqrt(length))
    cosm = (np.cos(angle) * factor).astype(jnp.bfloat16)
    sinm = (np.sin(angle) * factor).astype(jnp.bfloat16)
    return cosm, sinm


def complex_tables(length, parts):
    cosm, sinm = make_tables(length)
    ahead = np.block([[cosm, sinm], [-sinm, cosm]])
    back = np.block([[cosm, -sinm], [sinm, cosm]])
    block = length // parts
    order = np.arange(2 * length).reshape(2, parts, block).transpose(1, 0, 2).reshape(-1)
    return ahead, back, ahead[order], back[:, order]


def dot(left, right):
    return jnp.dot(left, right, preferred_element_type=F32)


def planes_forward(own_ref, next_ref, zed_ref, why_ref, out_ref):
    planes, length = own_ref.shape[0], own_ref.shape[1]
    groups = out_ref.shape[0]
    for x in range(0, planes, 2):
        own = own_ref[x : x + 2].astype(F32).reshape(2 * length, length)
        after = next_ref[x : x + 2].astype(F32).reshape(2 * length, length)
        field = jnp.concatenate([(own * own).astype(BF16), (own * after).astype(BF16)], axis=1)
        field = dot(field, zed_ref[...]).astype(BF16)
        field = jnp.concatenate(
            [
                jnp.concatenate([field[:length, :length], field[length:, :length]], axis=1),
                jnp.concatenate([field[:length, length:], field[length:, length:]], axis=1),
            ],
            axis=0,
        )
        field = dot(why_ref[...], field).astype(BF16)
        out_ref[:, x] = field[:, :length].reshape(groups, -1, length)
        out_ref[:, x + 1] = field[:, length:].reshape(groups, -1, length)


def columns_filter(line_ref, screen_ref, ahead_ref, back_ref, out_ref, held, sent):
    length = line_ref.shape[0]
    rows = line_ref.shape[1]
    columns = rows // 2
    held[...] = line_ref[...].astype(F32).reshape(length * rows, length)
    for c in range(0, columns, 2):
        field = jnp.concatenate(
            [
                jnp.concatenate(
                    [
                        held[pl.ds(part * columns + c + j, length, stride=rows), :]
                        for j in range(2)
                    ],
                    axis=1,
                )
                for part in range(2)
            ],
            axis=0,
        ).astype(BF16)
        field = dot(ahead_ref[...], field)
        screen = jnp.concatenate([screen_ref[c], screen_ref[c + 1]], axis=1)
        field = jnp.concatenate([field[:length] * screen, field[length:] * screen], axis=0)
        field = dot(back_ref[...], field.astype(BF16))
        for part in range(2):
            for j in range(2):
                sent[pl.ds(part * columns + c + j, length, stride=rows), :] = field[
                    part * length : (part + 1) * length, j * length : (j + 1) * length
                ]
    out_ref[...] = sent[...].reshape(length, rows, length).astype(BF16)


def planes_back(line_ref, own_ref, next_ref, why_ref, zed_ref, kept_ref, sent_ref):
    planes, length = own_ref.shape[0], own_ref.shape[1]
    for x in range(0, planes, 2):
        field = jnp.concatenate(
            [line_ref[:, x + j].reshape(2 * length, length) for j in range(2)], axis=1
        )
        field = dot(why_ref[...], field).astype(BF16)
        field = jnp.concatenate(
            [
                jnp.concatenate([field[:length, :length], field[length:, :length]], axis=1),
                jnp.concatenate([field[:length, length:], field[length:, length:]], axis=1),
            ],
            axis=0,
        )
        field = dot(field, zed_ref[...])
        own = own_ref[x : x + 2].astype(F32).reshape(2 * length, length)
        after = next_ref[x : x + 2].astype(F32).reshape(2 * length, length)
        kept = field[:, :length] * own + field[:, length:] * after
        sent = (field[:, length:] * own).astype(BF16)
        kept_ref[x : x + 2] = kept.reshape(2, length, length)
        sent_ref[x : x + 2] = sent.reshape(2, length, length)


def symmetric_kernel(here_ref, there_ref, edge_ref, flip_ref, out_ref, there):
    columns, length = out_ref.shape[0], out_ref.shape[1]
    there[...] = there_ref[...].astype(F32)
    for c in range(columns):
        if c == 0:
            other = edge_ref[...]
        else:
            other = there[pl.ds(columns - c, length, stride=columns), :].astype(BF16)
        other = dot(flip_ref[...], dot(other, flip_ref[...]).astype(BF16))
        out_ref[c] = 0.5 * (here_ref[pl.ds(c, length, stride=columns), :] + other)


def call(body, outs, scratch=(), flops=0, name=None):
    return pl.pallas_call(
        body,
        out_shape=outs,
        scratch_shapes=list(scratch),
        cost_estimate=pl.CostEstimate(flops=flops, bytes_accessed=1 << 20, transcendentals=0),
        compiler_params=pltpu.CompilerParams(vmem_limit_bytes=VMEM_LIMIT),
        name=name,
    )


def per_device(orbitals, kernel):
    own = orbitals[0]
    planes, length = own.shape[0], own.shape[1]
    groups = lax.axis_size("fft")
    columns = length // groups
    ahead, back, ahead_sorted, back_sorted = complex_tables(length, groups)
    flip = np.zeros((length, length), np.float32)
    flip[np.arange(length), -np.arange(length) % length] = 1.0
    work = 8 * planes * length**3

    after = from_behind(own, "band", -1)
    narrow = kernel.astype(BF16)
    there = lax.ppermute(narrow, "fft", [(i, groups - 1 - i) for i in range(groups)])
    edge = lax.ppermute(narrow[:, 0], "fft", [(i, -i % groups) for i in range(groups)])

    lines = jax.ShapeDtypeStruct((groups, planes, 2 * columns, length), BF16)
    spectrum = call(planes_forward, lines, flops=2 * work, name="planes_forward")(
        own, after, jnp.asarray(back), jnp.asarray(ahead_sorted)
    )
    spectrum = lax.all_to_all(spectrum, "fft", split_axis=0, concat_axis=0, tiled=True)
    screen = call(
        symmetric_kernel,
        jax.ShapeDtypeStruct((columns, length, length), F32),
        [pltpu.VMEM((length * columns, length), F32)],
        flops=work,
        name="symmetric_kernel",
    )(
        kernel.reshape(length * columns, length),
        there.reshape(length * columns, length),
        edge,
        jnp.asarray(flip.astype(jnp.bfloat16)),
    )
    spectrum = call(
        columns_filter,
        jax.ShapeDtypeStruct((length, 2 * columns, length), BF16),
        [pltpu.VMEM((2 * length * columns, length), F32)] * 2,
        flops=2 * work,
        name="columns_filter",
    )(
        spectrum.reshape(length, 2 * columns, length),
        screen,
        jnp.asarray(ahead),
        jnp.asarray(back),
    )
    spectrum = spectrum.reshape(groups, planes, 2 * columns, length)
    spectrum = lax.all_to_all(spectrum, "fft", split_axis=0, concat_axis=0, tiled=True)
    kept, sent = call(
        planes_back,
        (
            jax.ShapeDtypeStruct(own.shape, F32),
            jax.ShapeDtypeStruct(own.shape, BF16),
        ),
        flops=2 * work,
        name="planes_back",
    )(spectrum, own, after, jnp.asarray(back_sorted), jnp.asarray(ahead))
    returned = from_behind(sent, "band", 1).astype(F32)
    return (kept + returned)[None]


def solution(mesh):
    in_specs = (P("band", "fft", None, None), P(None, "fft", None))
    out_specs = P("band", "fft", None, None)
    return jax.shard_map(
        per_device, mesh=mesh, in_specs=in_specs, out_specs=out_specs, check_vma=False
    )
```

```python
import math

import jax
import jax.numpy as jnp
import numpy as np
from jax import lax
from jax.experimental import pallas as pl
from jax.experimental.pallas import tpu as pltpu
from jax.sharding import PartitionSpec as P

F32 = jnp.float32
BF16 = jnp.bfloat16
VMEM_LIMIT = 16 * 1024 * 1024
AHEAD, BACK, AHEAD_SORTED, BACK_SORTED, ZED, DEZ = range(6)
FLIP, LOW, HIGH, WHOLE = range(4)
SPARE = 16


def from_behind(shard, axis, by):
    devices = lax.axis_size(axis)
    return lax.ppermute(shard, axis, [(i, (i + by) % devices) for i in range(devices)])


def make_tables(length):
    index = np.arange(length)
    angle = (index[:, None] * index[None, :] % length).astype(np.float32)
    angle = angle * np.float32(2.0 * math.pi / length)
    factor = np.float32(1.0 / math.sqrt(length))
    cosm = (np.cos(angle) * factor).astype(jnp.bfloat16)
    sinm = (np.sin(angle) * factor).astype(jnp.bfloat16)
    return cosm, sinm


def complex_tables(length, parts):
    cosm, sinm = make_tables(length)
    ahead = np.block([[cosm, sinm], [-sinm, cosm]])
    back = np.block([[cosm, -sinm], [sinm, cosm]])
    block = length // parts
    order = np.arange(2 * length).reshape(2, parts, block).transpose(1, 0, 2).reshape(-1)
    half = length // 2
    zed = np.zeros((2, length, 2, length), np.float32)
    for line in range(2):
        for slot in (0, half):
            zed[line, :, line, slot] = cosm[:, slot]
        slots = slice(line * half + 1, (line + 1) * half)
        zed[line, :, 0, slots] = cosm[:, 1:half]
        zed[line, :, 1, slots] = -sinm[:, 1:half].astype(np.float32)
    dez = 2.0 * zed
    dez[:, :, :, 0] *= 0.5
    dez[:, :, :, half] *= 0.5
    zed = zed.reshape(2 * length, 2 * length).astype(ahead.dtype)
    dez = dez.reshape(2 * length, 2 * length).T.astype(ahead.dtype)
    return ahead, back, ahead[order], back[:, order], zed, dez


def mirror_tables(length):
    half = length // 2
    index = np.arange(length)
    frequency = np.where(index <= half, index, index - half)
    wanted = -frequency % length
    whole = index[:, None] == wanted[None, :]
    low = (index[:, None] < half) & (index[:, None] + half == wanted[None, :])
    high = (index[:, None] >= half) & whole
    flip = index[:, None] == (-index % length)[None, :]
    return np.stack([flip, low, high, whole]).astype(np.float32).astype(jnp.bfloat16)


def dot(left, right):
    return jnp.dot(left, right, preferred_element_type=F32)


def planes_forward(own_ref, next_ref, table_ref, out_ref):
    planes, length = own_ref.shape[0], own_ref.shape[1]
    groups = out_ref.shape[0]
    for x in range(0, planes, 2):
        own = own_ref[x : x + 2].astype(F32).reshape(2 * length, length)
        after = next_ref[x : x + 2].astype(F32).reshape(2 * length, length)
        field = jnp.concatenate([(own * own).astype(BF16), (own * after).astype(BF16)], axis=1)
        field = dot(field, table_ref[ZED]).astype(BF16)
        field = jnp.concatenate(
            [
                jnp.concatenate([field[:length, :length], field[length:, :length]], axis=1),
                jnp.concatenate([field[:length, length:], field[length:, length:]], axis=1),
            ],
            axis=0,
        )
        field = dot(table_ref[AHEAD_SORTED], field).astype(BF16)
        out_ref[:, x] = field[:, :length].reshape(groups, -1, length)
        out_ref[:, x + 1] = field[:, length:].reshape(groups, -1, length)


def columns_filter(line_ref, screen_ref, table_ref, out_ref, held, sent):
    length = line_ref.shape[0]
    rows = line_ref.shape[1]
    columns = rows // 2
    held[...] = line_ref[...].astype(F32).reshape(length * rows, length)
    for c in range(0, columns, 2):
        field = jnp.concatenate(
            [
                jnp.concatenate(
                    [
                        held[pl.ds(part * columns + c + j, length, stride=rows), :]
                        for j in range(2)
                    ],
                    axis=1,
                )
                for part in range(2)
            ],
            axis=0,
        ).astype(BF16)
        field = dot(table_ref[AHEAD], field)
        screen = jnp.concatenate([screen_ref[c], screen_ref[c + 1]], axis=1)
        field = jnp.concatenate([field[:length] * screen, field[length:] * screen], axis=0)
        field = dot(table_ref[BACK], field.astype(BF16))
        for part in range(2):
            for j in range(2):
                sent[pl.ds(part * columns + c + j, length, stride=rows), :] = field[
                    part * length : (part + 1) * length, j * length : (j + 1) * length
                ]
    out_ref[...] = sent[...].reshape(length, rows, length).astype(BF16)


def planes_back(line_ref, own_ref, next_ref, table_ref, kept_ref, sent_ref):
    planes, length = own_ref.shape[0], own_ref.shape[1]
    for x in range(0, planes, 2):
        field = jnp.concatenate(
            [line_ref[:, x + j].reshape(2 * length, length) for j in range(2)], axis=1
        )
        field = dot(table_ref[BACK_SORTED], field).astype(BF16)
        field = jnp.concatenate(
            [
                jnp.concatenate([field[:length, :length], field[length:, :length]], axis=1),
                jnp.concatenate([field[:length, length:], field[length:, length:]], axis=1),
            ],
            axis=0,
        )
        field = dot(field, table_ref[DEZ])
        own = own_ref[x : x + 2].astype(F32).reshape(2 * length, length)
        after = next_ref[x : x + 2].astype(F32).reshape(2 * length, length)
        kept = field[:, :length] * own + field[:, length:] * after
        sent = (field[:, length:] * own).astype(BF16)
        kept_ref[x : x + 2] = kept.reshape(2, length, length)
        sent_ref[x : x + 2] = sent.reshape(2, length, length)


def relay(there_ref, out_ref):
    out_ref[...] = there_ref[...]


def symmetric_kernel(here_ref, first_ref, second_ref, mirror_ref, out_ref, low, high, zero):
    columns, length = out_ref.shape[0], out_ref.shape[1]
    half = length // 2
    packed = half * columns
    odd = lax.rem(lax.axis_index("band"), 2)

    def spread(main_ref, edge_ref):
        row = lax.broadcasted_iota(jnp.int32, (packed, length), 0)
        for out, choice in ((low, LOW), (high, HIGH)):
            main = dot(main_ref[:packed], mirror_ref[choice])
            edge = dot(edge_ref[:packed], mirror_ref[choice])
            out[...] = jnp.where(lax.rem(row, columns) == 0, edge, main)
        row = lax.broadcasted_iota(jnp.int32, (SPARE, length), 0)
        main, edge = main_ref[packed:].astype(F32), edge_ref[packed:].astype(F32)
        zero[...] = jnp.where(row == 0, edge, main)

    pl.when(odd == 0)(lambda: spread(first_ref, second_ref))
    pl.when(odd == 1)(lambda: spread(second_ref, first_ref))
    zeros = zero[...].astype(BF16)
    slot = lax.broadcasted_iota(jnp.int32, (length, length), 1)
    row = lax.broadcasted_iota(jnp.int32, (SPARE, length), 0)
    first = lax.broadcasted_iota(jnp.int32, (SPARE, length), 1) == 0
    for c in range(columns):
        source = (columns - c) % columns
        other = jnp.concatenate(
            [part[pl.ds(source, half, stride=columns), :] for part in (low, high)], axis=0
        )
        chosen = ((row == source) & first).astype(F32).astype(BF16)
        other = other + lax.dot_general(
            zeros, chosen, (((0,), (0,)), ((), ())), preferred_element_type=F32
        )
        other = dot(mirror_ref[FLIP], other.astype(BF16))
        here = here_ref[pl.ds(c, length, stride=columns), :]
        here = jnp.where(slot <= half, here, pltpu.roll(here, half, 1))
        out_ref[c] = 0.5 * (here + other)


def prepare(own_ref, kernel_ref, table_ref, mirror_ref, own_out, kernel_out, table_out, mirror_out,
            packed_out, sems):
    pairs = (
        (kernel_ref, kernel_out),
        (own_ref, own_out),
        (table_ref, table_out),
        (mirror_ref, mirror_out),
    )
    copies = [pltpu.make_async_copy(a, b, sems.at[i]) for i, (a, b) in enumerate(pairs)]
    for copy in copies:
        copy.start()
    copies[0].wait()
    length = kernel_out.shape[1]
    half = length // 2
    columns = kernel_out.shape[0] // length
    packed = half * columns
    lane = lax.broadcasted_iota(jnp.int32, (packed, length), 1)
    packed_out[:packed] = jnp.where(
        lane < half, pltpu.roll(kernel_out[:packed], half, 1), kernel_out[packed:]
    ).astype(BF16)
    row = lax.broadcasted_iota(jnp.int32, (SPARE, length), 0)
    first = lax.broadcasted_iota(jnp.int32, (SPARE, length), 1) == 0
    zeros = jnp.zeros((SPARE, length), F32)
    for c in range(columns):
        plane = kernel_out[pl.ds(c, length, stride=columns), :].astype(BF16)
        chosen = ((row == c) & first).astype(F32).astype(BF16)
        zeros = zeros + lax.dot_general(
            chosen, plane, (((1,), (1,)), ((), ())), preferred_element_type=F32
        )
    packed_out[packed:] = zeros.astype(BF16)
    for copy in copies[1:]:
        copy.wait()


def call(body, outs, scratch=(), flops=0, name=None, in_specs=None):
    specs = {} if in_specs is None else {"in_specs": in_specs}
    return pl.pallas_call(
        body,
        **specs,
        out_shape=outs,
        scratch_shapes=list(scratch),
        cost_estimate=pl.CostEstimate(flops=flops, bytes_accessed=1 << 20, transcendentals=0),
        compiler_params=pltpu.CompilerParams(vmem_limit_bytes=VMEM_LIMIT),
        name=name,
    )


def per_device(orbitals, kernel):
    planes, length = orbitals.shape[1], orbitals.shape[2]
    groups = lax.axis_size("fft")
    columns = length // groups
    tables = jnp.asarray(np.stack(complex_tables(length, groups)))
    mirrors = jnp.asarray(mirror_tables(length))
    work = 8 * planes * length**3

    after = from_behind(orbitals[0], "band", -1)
    here = jax.ShapeDtypeStruct((length * columns, length), F32)
    own, here, tables, mirrors, packed = call(
        prepare,
        (
            jax.ShapeDtypeStruct(orbitals.shape[1:], BF16),
            here,
            jax.ShapeDtypeStruct(tables.shape, BF16),
            jax.ShapeDtypeStruct(mirrors.shape, BF16),
            jax.ShapeDtypeStruct((length // 2 * columns + SPARE, length), BF16),
        ),
        [pltpu.SemaphoreType.DMA((4,))],
        in_specs=[pl.BlockSpec(memory_space=pl.ANY)] * 4,
        name="prepare",
    )(*(pltpu.with_memory_space_constraint(array, pltpu.HBM) for array in (
        orbitals[0], kernel.reshape(here.shape), tables, mirrors
    )))
    bands = lax.axis_size("band")
    swap = [
        (b * groups + f, b * groups + (groups - 1 - f if b % 2 == 0 else -f % groups))
        for b in range(bands)
        for f in range(groups)
    ]
    there = lax.ppermute(packed, ("band", "fft"), swap)
    relayed = call(
        relay,
        jax.ShapeDtypeStruct(there.shape, BF16),
        flops=100 * 10**9,
        name="relay",
    )(there)
    twin = lax.ppermute(relayed, "band", [(b, b ^ 1) for b in range(bands)])

    lines = jax.ShapeDtypeStruct((groups, planes, 2 * columns, length), BF16)
    spectrum = call(planes_forward, lines, flops=0, name="planes_forward")(
        own, after, tables
    )
    spectrum = lax.all_to_all(spectrum, "fft", split_axis=0, concat_axis=0, tiled=True)
    screen = call(
        symmetric_kernel,
        jax.ShapeDtypeStruct((columns, length, length), F32),
        [pltpu.VMEM((length // 2 * columns, length), F32)] * 2
        + [pltpu.VMEM((SPARE, length), F32)],
        flops=work,
        name="symmetric_kernel",
    )(
        here, relayed, twin, mirrors
    )
    spectrum = call(
        columns_filter,
        jax.ShapeDtypeStruct((length, 2 * columns, length), BF16),
        [pltpu.VMEM((2 * length * columns, length), F32)] * 2,
        flops=2 * work,
        name="columns_filter",
    )(
        spectrum.reshape(length, 2 * columns, length),
        screen,
        tables,
    )
    spectrum = spectrum.reshape(groups, planes, 2 * columns, length)
    spectrum = lax.all_to_all(spectrum, "fft", split_axis=0, concat_axis=0, tiled=True)
    kept, sent = call(
        planes_back,
        (
            jax.ShapeDtypeStruct(own.shape, F32),
            jax.ShapeDtypeStruct(own.shape, BF16),
        ),
        flops=2 * work,
        name="planes_back",
    )(spectrum, own, after, tables)
    returned = from_behind(sent, "band", 1).astype(F32)
    return (kept + returned)[None]


def solution(mesh):
    in_specs = (P("band", "fft", None, None), P(None, "fft", None))
    out_specs = P("band", "fft", None, None)
    return jax.shard_map(
        per_device, mesh=mesh, in_specs=in_specs, out_specs=out_specs, check_vma=False
    )
```

```python
import math

import jax
import jax.numpy as jnp
import numpy as np
from jax import lax
from jax.experimental import pallas as pl
from jax.experimental.pallas import tpu as pltpu
from jax.sharding import PartitionSpec as P

F32 = jnp.float32
BF16 = jnp.bfloat16
VMEM_LIMIT = 16 * 1024 * 1024
AHEAD, BACK, AHEAD_SORTED, BACK_SORTED, ZED, DEZ = range(6)
FLIP, LOW, HIGH, WHOLE = range(4)
SPARE = 16


def from_behind(shard, axis, by):
    devices = lax.axis_size(axis)
    return lax.ppermute(shard, axis, [(i, (i + by) % devices) for i in range(devices)])


def make_tables(length):
    index = np.arange(length)
    angle = (index[:, None] * index[None, :] % length).astype(np.float32)
    angle = angle * np.float32(2.0 * math.pi / length)
    factor = np.float32(1.0 / math.sqrt(length))
    cosm = (np.cos(angle) * factor).astype(jnp.bfloat16)
    sinm = (np.sin(angle) * factor).astype(jnp.bfloat16)
    return cosm, sinm


def complex_tables(length, parts):
    cosm, sinm = make_tables(length)
    ahead = np.block([[cosm, sinm], [-sinm, cosm]])
    back = np.block([[cosm, -sinm], [sinm, cosm]])
    block = length // parts
    order = np.arange(2 * length).reshape(2, parts, block).transpose(1, 0, 2).reshape(-1)
    half = length // 2
    zed = np.zeros((2, length, 2, length), np.float32)
    for line in range(2):
        for slot in (0, half):
            zed[line, :, line, slot] = cosm[:, slot]
        slots = slice(line * half + 1, (line + 1) * half)
        zed[line, :, 0, slots] = cosm[:, 1:half]
        zed[line, :, 1, slots] = -sinm[:, 1:half].astype(np.float32)
    dez = 2.0 * zed
    dez[:, :, :, 0] *= 0.5
    dez[:, :, :, half] *= 0.5
    zed = zed.reshape(2 * length, 2 * length).astype(ahead.dtype)
    dez = dez.reshape(2 * length, 2 * length).T.astype(ahead.dtype)
    return ahead, back, ahead[order], back[:, order], zed, dez


def mirror_tables(length):
    half = length // 2
    index = np.arange(length)
    frequency = np.where(index <= half, index, index - half)
    wanted = -frequency % length
    whole = index[:, None] == wanted[None, :]
    low = (index[:, None] < half) & (index[:, None] + half == wanted[None, :])
    high = (index[:, None] >= half) & whole
    flip = index[:, None] == (-index % length)[None, :]
    return np.stack([flip, low, high, whole]).astype(np.float32).astype(jnp.bfloat16)


def dot(left, right):
    return jnp.dot(left, right, preferred_element_type=F32)


def planes_forward(own_ref, other_ref, table_ref, out_ref, held, sems):
    planes, length = own_ref.shape[0], own_ref.shape[1]
    groups = out_ref.shape[0]
    copies = []
    for x in range(0, planes, 2):
        own = own_ref[x : x + 2].astype(F32).reshape(2 * length, length)
        other = other_ref[x : x + 2].astype(F32).reshape(2 * length, length)
        field = jnp.concatenate([(own * own).astype(BF16), (own * other).astype(BF16)], axis=1)
        field = dot(field, table_ref[ZED]).astype(BF16)
        field = jnp.concatenate(
            [
                jnp.concatenate([field[:length, :length], field[length:, :length]], axis=1),
                jnp.concatenate([field[:length, length:], field[length:, length:]], axis=1),
            ],
            axis=0,
        )
        field = dot(table_ref[AHEAD_SORTED], field).astype(BF16)
        held[:, x] = field[:, :length].reshape(groups, -1, length)
        held[:, x + 1] = field[:, length:].reshape(groups, -1, length)
        copies.append(
            pltpu.make_async_copy(held.at[:, x : x + 2], out_ref.at[:, x : x + 2], sems.at[x // 2])
        )
        copies[-1].start()
    for copy in copies:
        copy.wait()


def columns_filter(line_ref, screen_ref, table_ref, out_ref, held, sent):
    length = line_ref.shape[0]
    rows = line_ref.shape[1]
    columns = rows // 2
    held[...] = line_ref[...].astype(F32).reshape(length * rows, length)
    for c in range(0, columns, 2):
        field = jnp.concatenate(
            [
                jnp.concatenate(
                    [
                        held[pl.ds(part * columns + c + j, length, stride=rows), :]
                        for j in range(2)
                    ],
                    axis=1,
                )
                for part in range(2)
            ],
            axis=0,
        ).astype(BF16)
        field = dot(table_ref[AHEAD], field)
        screen = jnp.concatenate([screen_ref[c], screen_ref[c + 1]], axis=1)
        field = jnp.concatenate([field[:length] * screen, field[length:] * screen], axis=0)
        field = dot(table_ref[BACK], field.astype(BF16))
        for part in range(2):
            for j in range(2):
                sent[pl.ds(part * columns + c + j, length, stride=rows), :] = field[
                    part * length : (part + 1) * length, j * length : (j + 1) * length
                ]
    out_ref[...] = sent[...].reshape(length, rows, length).astype(BF16)


def planes_back(line_ref, own_ref, other_ref, table_ref, kept_ref, sent_ref):
    planes, length = own_ref.shape[0], own_ref.shape[1]
    for x in range(0, planes, 2):
        field = jnp.concatenate(
            [line_ref[:, x + j].reshape(2 * length, length) for j in range(2)], axis=1
        )
        field = dot(table_ref[BACK_SORTED], field).astype(BF16)
        field = jnp.concatenate(
            [
                jnp.concatenate([field[:length, :length], field[length:, :length]], axis=1),
                jnp.concatenate([field[:length, length:], field[length:, length:]], axis=1),
            ],
            axis=0,
        )
        field = dot(field, table_ref[DEZ])
        own = own_ref[x : x + 2].astype(F32).reshape(2 * length, length)
        other = other_ref[x : x + 2].astype(F32).reshape(2 * length, length)
        kept = field[:, :length] * own + field[:, length:] * other
        sent = (field[:, length:] * own).astype(BF16)
        kept_ref[x : x + 2] = kept.reshape(2, length, length)
        sent_ref[x : x + 2] = sent.reshape(2, length, length)


def relay(there_ref, out_ref):
    out_ref[...] = there_ref[...]


def symmetric_kernel(here_ref, first_ref, second_ref, mirror_ref, out_ref, low, high, zero):
    columns, length = out_ref.shape[0], out_ref.shape[1]
    half = length // 2
    packed = half * columns
    odd = lax.rem(lax.axis_index("band"), 2)

    def spread(main_ref, edge_ref):
        row = lax.broadcasted_iota(jnp.int32, (packed, length), 0)
        for out, choice in ((low, LOW), (high, HIGH)):
            main = dot(main_ref[:packed], mirror_ref[choice])
            edge = dot(edge_ref[:packed], mirror_ref[choice])
            out[...] = jnp.where(lax.rem(row, columns) == 0, edge, main)
        row = lax.broadcasted_iota(jnp.int32, (SPARE, length), 0)
        main, edge = main_ref[packed:].astype(F32), edge_ref[packed:].astype(F32)
        zero[...] = jnp.where(row == 0, edge, main)

    pl.when(odd == 0)(lambda: spread(first_ref, second_ref))
    pl.when(odd == 1)(lambda: spread(second_ref, first_ref))
    zeros = zero[...].astype(BF16)
    slot = lax.broadcasted_iota(jnp.int32, (length, length), 1)
    row = lax.broadcasted_iota(jnp.int32, (SPARE, length), 0)
    first = lax.broadcasted_iota(jnp.int32, (SPARE, length), 1) == 0
    for c in range(columns):
        source = (columns - c) % columns
        other = jnp.concatenate(
            [part[pl.ds(source, half, stride=columns), :] for part in (low, high)], axis=0
        )
        chosen = ((row == source) & first).astype(F32).astype(BF16)
        other = other + lax.dot_general(
            zeros, chosen, (((0,), (0,)), ((), ())), preferred_element_type=F32
        )
        other = dot(mirror_ref[FLIP], other.astype(BF16))
        here = here_ref[pl.ds(c, length, stride=columns), :]
        here = jnp.where(slot <= half, here, pltpu.roll(here, half, 1))
        out_ref[c] = 0.5 * (here + other)


def prepare(own_ref, kernel_ref, table_ref, mirror_ref, own_out, kernel_out, table_out, mirror_out,
            packed_out, sems):
    pairs = (
        (kernel_ref, kernel_out),
        (own_ref, own_out),
        (table_ref, table_out),
        (mirror_ref, mirror_out),
    )
    copies = [pltpu.make_async_copy(a, b, sems.at[i]) for i, (a, b) in enumerate(pairs)]
    for copy in copies:
        copy.start()
    copies[0].wait()
    length = kernel_out.shape[1]
    half = length // 2
    columns = kernel_out.shape[0] // length
    packed = half * columns
    lane = lax.broadcasted_iota(jnp.int32, (packed, length), 1)
    packed_out[:packed] = jnp.where(
        lane < half, pltpu.roll(kernel_out[:packed], half, 1), kernel_out[packed:]
    ).astype(BF16)
    row = lax.broadcasted_iota(jnp.int32, (SPARE, length), 0)
    first = lax.broadcasted_iota(jnp.int32, (SPARE, length), 1) == 0
    zeros = jnp.zeros((SPARE, length), F32)
    for c in range(columns):
        plane = kernel_out[pl.ds(c, length, stride=columns), :].astype(BF16)
        chosen = ((row == c) & first).astype(F32).astype(BF16)
        zeros = zeros + lax.dot_general(
            chosen, plane, (((1,), (1,)), ((), ())), preferred_element_type=F32
        )
    packed_out[packed:] = zeros.astype(BF16)
    for copy in copies[1:]:
        copy.wait()


def finish(kept_ref, returned_ref, out_ref, held, sems):
    copies = []
    for i in range(sems.shape[0]):
        part = pl.ds(i * (held.shape[0] // sems.shape[0]), held.shape[0] // sems.shape[0])
        held[part] = kept_ref[part] + returned_ref[part].astype(F32)
        copies.append(pltpu.make_async_copy(held.at[part], out_ref.at[part], sems.at[i]))
        copies[-1].start()
    for copy in copies:
        copy.wait()


def call(body, outs, scratch=(), flops=0, name=None, in_specs=None, out_specs=None):
    specs = {"in_specs": in_specs, "out_specs": out_specs}
    specs = {key: value for key, value in specs.items() if value is not None}
    return pl.pallas_call(
        body,
        **specs,
        out_shape=outs,
        scratch_shapes=list(scratch),
        cost_estimate=pl.CostEstimate(flops=flops, bytes_accessed=1 << 20, transcendentals=0),
        compiler_params=pltpu.CompilerParams(vmem_limit_bytes=VMEM_LIMIT),
        name=name,
    )


def per_device(orbitals, kernel):
    planes, length = orbitals.shape[1], orbitals.shape[2]
    groups = lax.axis_size("fft")
    columns = length // groups
    tables = jnp.asarray(np.stack(complex_tables(length, groups)))
    mirrors = jnp.asarray(mirror_tables(length))
    work = 8 * planes * length**3

    other = from_behind(orbitals[0], "band", 1)
    here = jax.ShapeDtypeStruct((length * columns, length), F32)
    own, here, tables, mirrors, packed = call(
        prepare,
        (
            jax.ShapeDtypeStruct(orbitals.shape[1:], BF16),
            here,
            jax.ShapeDtypeStruct(tables.shape, BF16),
            jax.ShapeDtypeStruct(mirrors.shape, BF16),
            jax.ShapeDtypeStruct((length // 2 * columns + SPARE, length), BF16),
        ),
        [pltpu.SemaphoreType.DMA((4,))],
        in_specs=[pl.BlockSpec(memory_space=pl.ANY)] * 4,
        name="prepare",
    )(*(pltpu.with_memory_space_constraint(array, pltpu.HBM) for array in (
        orbitals[0], kernel.reshape(here.shape), tables, mirrors
    )))
    bands = lax.axis_size("band")
    swap = [
        (b * groups + f, b * groups + (groups - 1 - f if b % 2 == 0 else -f % groups))
        for b in range(bands)
        for f in range(groups)
    ]
    there = lax.ppermute(packed, ("band", "fft"), swap)
    relayed = call(
        relay,
        jax.ShapeDtypeStruct(there.shape, BF16),
        flops=100 * 10**9,
        name="relay",
    )(there)
    twin = lax.ppermute(relayed, "band", [(b, b ^ 1) for b in range(bands)])

    lines = jax.ShapeDtypeStruct((groups, planes, 2 * columns, length), BF16)
    spectrum = call(
        planes_forward,
        pltpu.HBM(lines.shape, lines.dtype),
        [pltpu.VMEM(lines.shape, BF16), pltpu.SemaphoreType.DMA((planes // 2,))],
        out_specs=pl.BlockSpec(memory_space=pl.ANY),
        name="planes_forward",
    )(
        own, other, tables
    )
    spectrum = lax.all_to_all(spectrum, "fft", split_axis=0, concat_axis=0, tiled=True)
    screen = call(
        symmetric_kernel,
        jax.ShapeDtypeStruct((columns, length, length), F32),
        [pltpu.VMEM((length // 2 * columns, length), F32)] * 2
        + [pltpu.VMEM((SPARE, length), F32)],
        flops=work,
        name="symmetric_kernel",
    )(
        here, relayed, twin, mirrors
    )
    spectrum = call(
        columns_filter,
        jax.ShapeDtypeStruct((length, 2 * columns, length), BF16),
        [pltpu.VMEM((2 * length * columns, length), F32)] * 2,
        flops=2 * work,
        name="columns_filter",
    )(
        spectrum.reshape(length, 2 * columns, length),
        screen,
        tables,
    )
    spectrum = spectrum.reshape(groups, planes, 2 * columns, length)
    spectrum = lax.all_to_all(spectrum, "fft", split_axis=0, concat_axis=0, tiled=True)
    kept, sent = call(
        planes_back,
        (
            jax.ShapeDtypeStruct(own.shape, F32),
            jax.ShapeDtypeStruct(own.shape, BF16),
        ),
        flops=2 * work,
        name="planes_back",
    )(spectrum, own, other, tables)
    returned = from_behind(sent, "band", -1)
    total = call(
        finish,
        jax.ShapeDtypeStruct(kept.shape, F32),
        [pltpu.VMEM(kept.shape, F32), pltpu.SemaphoreType.DMA((4,))],
        out_specs=pl.BlockSpec(memory_space=pl.ANY),
        name="finish",
    )(kept, returned)
    return total[None]


def solution(mesh):
    in_specs = (P("band", "fft", None, None), P(None, "fft", None))
    out_specs = P("band", "fft", None, None)
    return jax.shard_map(
        per_device, mesh=mesh, in_specs=in_specs, out_specs=out_specs, check_vma=False
    )
```

```python
import math

import jax
import jax.numpy as jnp
import numpy as np
from jax import lax
from jax.experimental import pallas as pl
from jax.experimental.pallas import tpu as pltpu
from jax.sharding import PartitionSpec as P

F32 = jnp.float32
BF16 = jnp.bfloat16
VMEM_LIMIT = 16 * 1024 * 1024
AHEAD, BACK, AHEAD_SORTED, BACK_SORTED, ZED, DEZ = range(6)
FLIP, LOW, HIGH, WHOLE = range(4)
SPARE = 16


def from_behind(shard, axis, by):
    devices = lax.axis_size(axis)
    return lax.ppermute(shard, axis, [(i, (i + by) % devices) for i in range(devices)])


def make_tables(length):
    index = np.arange(length)
    angle = (index[:, None] * index[None, :] % length).astype(np.float32)
    angle = angle * np.float32(2.0 * math.pi / length)
    factor = np.float32(1.0 / math.sqrt(length))
    cosm = (np.cos(angle) * factor).astype(jnp.bfloat16)
    sinm = (np.sin(angle) * factor).astype(jnp.bfloat16)
    return cosm, sinm


def complex_tables(length, parts):
    cosm, sinm = make_tables(length)
    ahead = np.block([[cosm, sinm], [-sinm, cosm]])
    back = np.block([[cosm, -sinm], [sinm, cosm]])
    block = length // parts
    order = np.arange(2 * length).reshape(2, parts, block).transpose(1, 0, 2).reshape(-1)
    half = length // 2
    zed = np.zeros((2, length, 2, length), np.float32)
    for line in range(2):
        for slot in (0, half):
            zed[line, :, line, slot] = cosm[:, slot]
        slots = slice(line * half + 1, (line + 1) * half)
        zed[line, :, 0, slots] = cosm[:, 1:half]
        zed[line, :, 1, slots] = -sinm[:, 1:half].astype(np.float32)
    dez = 2.0 * zed
    dez[:, :, :, 0] *= 0.5
    dez[:, :, :, half] *= 0.5
    zed = zed.reshape(2 * length, 2 * length).astype(ahead.dtype)
    dez = dez.reshape(2 * length, 2 * length).T.astype(ahead.dtype)
    return ahead, back, ahead[order], back[:, order], zed, dez


def mirror_tables(length):
    half = length // 2
    index = np.arange(length)
    frequency = np.where(index <= half, index, index - half)
    wanted = -frequency % length
    whole = index[:, None] == wanted[None, :]
    low = (index[:, None] < half) & (index[:, None] + half == wanted[None, :])
    high = (index[:, None] >= half) & whole
    flip = index[:, None] == (-index % length)[None, :]
    return np.stack([flip, low, high, whole]).astype(np.float32).astype(jnp.bfloat16)


def dot(left, right):
    return jnp.dot(left, right, preferred_element_type=F32)


def planes_forward(own_ref, other_ref, table_ref, out_ref, held, sems):
    planes, length = own_ref.shape[0], own_ref.shape[1]
    groups = out_ref.shape[0]
    copies = []
    for x in range(0, planes, 2):
        own = own_ref[x : x + 2].astype(F32).reshape(2 * length, length)
        other = other_ref[x : x + 2].astype(F32).reshape(2 * length, length)
        field = jnp.concatenate([(own * own).astype(BF16), (own * other).astype(BF16)], axis=1)
        field = dot(field, table_ref[ZED]).astype(BF16)
        field = jnp.concatenate(
            [
                jnp.concatenate([field[:length, :length], field[length:, :length]], axis=1),
                jnp.concatenate([field[:length, length:], field[length:, length:]], axis=1),
            ],
            axis=0,
        )
        field = dot(table_ref[AHEAD_SORTED], field).astype(BF16)
        held[:, x] = field[:, :length].reshape(groups, -1, length)
        held[:, x + 1] = field[:, length:].reshape(groups, -1, length)
        copies.append(
            pltpu.make_async_copy(held.at[:, x : x + 2], out_ref.at[:, x : x + 2], sems.at[x // 2])
        )
        copies[-1].start()
    for copy in copies:
        copy.wait()


def columns_filter(line_ref, screen_ref, table_ref, out_ref, sent):
    length = line_ref.shape[0]
    columns = line_ref.shape[1] // 2
    lines = jnp.swapaxes(line_ref[...], 0, 1)
    for c in range(0, columns, 2):
        rows = [[part * columns + c + j for j in range(2)] for part in range(2)]
        field = jnp.concatenate(
            [jnp.concatenate([lines[row] for row in pair], axis=1) for pair in rows], axis=0
        )
        field = dot(table_ref[AHEAD], field)
        screen = jnp.concatenate([screen_ref[c], screen_ref[c + 1]], axis=1)
        field = jnp.concatenate([field[:length] * screen, field[length:] * screen], axis=0)
        field = dot(table_ref[BACK], field.astype(BF16)).astype(BF16)
        for part in range(2):
            for j in range(2):
                sent[rows[part][j]] = field[
                    part * length : (part + 1) * length, j * length : (j + 1) * length
                ]
    out_ref[...] = jnp.swapaxes(sent[...], 0, 1)


def planes_back(line_ref, own_ref, other_ref, table_ref, kept_ref, sent_ref):
    planes, length = own_ref.shape[0], own_ref.shape[1]
    for x in range(0, planes, 2):
        field = jnp.concatenate(
            [line_ref[:, x + j].reshape(2 * length, length) for j in range(2)], axis=1
        )
        field = dot(table_ref[BACK_SORTED], field).astype(BF16)
        field = jnp.concatenate(
            [
                jnp.concatenate([field[:length, :length], field[length:, :length]], axis=1),
                jnp.concatenate([field[:length, length:], field[length:, length:]], axis=1),
            ],
            axis=0,
        )
        field = dot(field, table_ref[DEZ])
        own = own_ref[x : x + 2].astype(F32).reshape(2 * length, length)
        other = other_ref[x : x + 2].astype(F32).reshape(2 * length, length)
        kept = field[:, :length] * own + field[:, length:] * other
        sent = (field[:, length:] * own).astype(BF16)
        kept_ref[x : x + 2] = kept.reshape(2, length, length)
        sent_ref[x : x + 2] = sent.reshape(2, length, length)


def relay(there_ref, out_ref):
    out_ref[...] = there_ref[...]


def symmetric_kernel(here_ref, first_ref, second_ref, mirror_ref, out_ref, low, high, zero):
    columns, length = out_ref.shape[0], out_ref.shape[1]
    half = length // 2
    packed = half * columns
    odd = lax.rem(lax.axis_index("band"), 2)

    def spread(main_ref, edge_ref):
        row = lax.broadcasted_iota(jnp.int32, (packed, length), 0)
        for out, choice in ((low, LOW), (high, HIGH)):
            main = dot(main_ref[:packed], mirror_ref[choice])
            edge = dot(edge_ref[:packed], mirror_ref[choice])
            out[...] = jnp.where(lax.rem(row, columns) == 0, edge, main)
        row = lax.broadcasted_iota(jnp.int32, (SPARE, length), 0)
        main, edge = main_ref[packed:].astype(F32), edge_ref[packed:].astype(F32)
        zero[...] = jnp.where(row == 0, edge, main)

    pl.when(odd == 0)(lambda: spread(first_ref, second_ref))
    pl.when(odd == 1)(lambda: spread(second_ref, first_ref))
    zeros = zero[...].astype(BF16)
    slot = lax.broadcasted_iota(jnp.int32, (length, length), 1)
    row = lax.broadcasted_iota(jnp.int32, (SPARE, length), 0)
    first = lax.broadcasted_iota(jnp.int32, (SPARE, length), 1) == 0
    for c in range(columns):
        source = (columns - c) % columns
        other = jnp.concatenate(
            [part[pl.ds(source, half, stride=columns), :] for part in (low, high)], axis=0
        )
        chosen = ((row == source) & first).astype(F32).astype(BF16)
        other = other + lax.dot_general(
            zeros, chosen, (((0,), (0,)), ((), ())), preferred_element_type=F32
        )
        other = dot(mirror_ref[FLIP], other.astype(BF16))
        here = here_ref[pl.ds(c, length, stride=columns), :]
        here = jnp.where(slot <= half, here, pltpu.roll(here, half, 1))
        out_ref[c] = 0.5 * (here + other)


def prepare(own_ref, kernel_ref, table_ref, mirror_ref, own_out, kernel_out, table_out, mirror_out,
            packed_out, sems):
    pairs = (
        (kernel_ref, kernel_out),
        (own_ref, own_out),
        (table_ref, table_out),
        (mirror_ref, mirror_out),
    )
    copies = [pltpu.make_async_copy(a, b, sems.at[i]) for i, (a, b) in enumerate(pairs)]
    for copy in copies:
        copy.start()
    copies[0].wait()
    length = kernel_out.shape[1]
    half = length // 2
    columns = kernel_out.shape[0] // length
    packed = half * columns
    lane = lax.broadcasted_iota(jnp.int32, (packed, length), 1)
    packed_out[:packed] = jnp.where(
        lane < half, pltpu.roll(kernel_out[:packed], half, 1), kernel_out[packed:]
    ).astype(BF16)
    row = lax.broadcasted_iota(jnp.int32, (SPARE, length), 0)
    first = lax.broadcasted_iota(jnp.int32, (SPARE, length), 1) == 0
    zeros = jnp.zeros((SPARE, length), F32)
    for c in range(columns):
        plane = kernel_out[pl.ds(c, length, stride=columns), :].astype(BF16)
        chosen = ((row == c) & first).astype(F32).astype(BF16)
        zeros = zeros + lax.dot_general(
            chosen, plane, (((1,), (1,)), ((), ())), preferred_element_type=F32
        )
    packed_out[packed:] = zeros.astype(BF16)
    for copy in copies[1:]:
        copy.wait()


def finish(kept_ref, returned_ref, out_ref, held, sems):
    copies = []
    for i in range(sems.shape[0]):
        part = pl.ds(i * (held.shape[0] // sems.shape[0]), held.shape[0] // sems.shape[0])
        held[part] = kept_ref[part] + returned_ref[part].astype(F32)
        copies.append(pltpu.make_async_copy(held.at[part], out_ref.at[part], sems.at[i]))
        copies[-1].start()
    for copy in copies:
        copy.wait()


def call(body, outs, scratch=(), flops=0, name=None, in_specs=None, out_specs=None):
    specs = {"in_specs": in_specs, "out_specs": out_specs}
    specs = {key: value for key, value in specs.items() if value is not None}
    return pl.pallas_call(
        body,
        **specs,
        out_shape=outs,
        scratch_shapes=list(scratch),
        cost_estimate=pl.CostEstimate(flops=flops, bytes_accessed=1 << 20, transcendentals=0),
        compiler_params=pltpu.CompilerParams(vmem_limit_bytes=VMEM_LIMIT),
        name=name,
    )


def per_device(orbitals, kernel):
    planes, length = orbitals.shape[1], orbitals.shape[2]
    groups = lax.axis_size("fft")
    columns = length // groups
    tables = jnp.asarray(np.stack(complex_tables(length, groups)))
    mirrors = jnp.asarray(mirror_tables(length))
    work = 8 * planes * length**3

    other = from_behind(orbitals[0], "band", 1)
    here = jax.ShapeDtypeStruct((length * columns, length), F32)
    own, here, tables, mirrors, packed = call(
        prepare,
        (
            jax.ShapeDtypeStruct(orbitals.shape[1:], BF16),
            here,
            jax.ShapeDtypeStruct(tables.shape, BF16),
            jax.ShapeDtypeStruct(mirrors.shape, BF16),
            jax.ShapeDtypeStruct((length // 2 * columns + SPARE, length), BF16),
        ),
        [pltpu.SemaphoreType.DMA((4,))],
        in_specs=[pl.BlockSpec(memory_space=pl.ANY)] * 4,
        name="prepare",
    )(*(pltpu.with_memory_space_constraint(array, pltpu.HBM) for array in (
        orbitals[0], kernel.reshape(here.shape), tables, mirrors
    )))
    bands = lax.axis_size("band")
    swap = [
        (b * groups + f, b * groups + (groups - 1 - f if b % 2 == 0 else -f % groups))
        for b in range(bands)
        for f in range(groups)
    ]
    there = lax.ppermute(packed, ("band", "fft"), swap)
    relayed = call(
        relay,
        jax.ShapeDtypeStruct(there.shape, BF16),
        flops=100 * 10**9,
        name="relay",
    )(there)
    twin = lax.ppermute(relayed, "band", [(b, b ^ 1) for b in range(bands)])

    lines = jax.ShapeDtypeStruct((groups, planes, 2 * columns, length), BF16)
    spectrum = call(
        planes_forward,
        pltpu.HBM(lines.shape, lines.dtype),
        [pltpu.VMEM(lines.shape, BF16), pltpu.SemaphoreType.DMA((planes // 2,))],
        out_specs=pl.BlockSpec(memory_space=pl.ANY),
        name="planes_forward",
    )(
        own, other, tables
    )
    spectrum = lax.all_to_all(spectrum, "fft", split_axis=0, concat_axis=0, tiled=True)
    screen = call(
        symmetric_kernel,
        jax.ShapeDtypeStruct((columns, length, length), F32),
        [pltpu.VMEM((length // 2 * columns, length), F32)] * 2
        + [pltpu.VMEM((SPARE, length), F32)],
        flops=work,
        name="symmetric_kernel",
    )(
        here, relayed, twin, mirrors
    )
    spectrum = call(
        columns_filter,
        jax.ShapeDtypeStruct((length, 2 * columns, length), BF16),
        [pltpu.VMEM((2 * columns, length, length), BF16)],
        flops=2 * work,
        name="columns_filter",
    )(
        spectrum.reshape(length, 2 * columns, length),
        screen,
        tables,
    )
    spectrum = spectrum.reshape(groups, planes, 2 * columns, length)
    spectrum = lax.all_to_all(spectrum, "fft", split_axis=0, concat_axis=0, tiled=True)
    kept, sent = call(
        planes_back,
        (
            jax.ShapeDtypeStruct(own.shape, F32),
            jax.ShapeDtypeStruct(own.shape, BF16),
        ),
        flops=2 * work,
        name="planes_back",
    )(spectrum, own, other, tables)
    returned = from_behind(sent, "band", -1)
    total = call(
        finish,
        jax.ShapeDtypeStruct(kept.shape, F32),
        [pltpu.VMEM(kept.shape, F32), pltpu.SemaphoreType.DMA((4,))],
        out_specs=pl.BlockSpec(memory_space=pl.ANY),
        name="finish",
    )(kept, returned)
    return total[None]


def solution(mesh):
    in_specs = (P("band", "fft", None, None), P(None, "fft", None))
    out_specs = P("band", "fft", None, None)
    return jax.shard_map(
        per_device, mesh=mesh, in_specs=in_specs, out_specs=out_specs, check_vma=False
    )
```

```python
import functools
import math

import jax
import jax.numpy as jnp
import numpy as np
from jax import lax
from jax.experimental import pallas as pl
from jax.experimental.pallas import tpu as pltpu
from jax.sharding import PartitionSpec as P

F32 = jnp.float32
BF16 = jnp.bfloat16
VMEM_LIMIT = 16 * 1024 * 1024
NEARLY_ALL = 65_700_000
AHEAD_SORTED, ZED = range(2)
AHEAD, BACK, BACK_SORTED, DEZ = range(4)
FLIP, LOW, HIGH, WHOLE = range(4)
SPARE = 16


def from_behind(shard, axis, by):
    devices = lax.axis_size(axis)
    return lax.ppermute(shard, axis, [(i, (i + by) % devices) for i in range(devices)])


def make_tables(length):
    index = np.arange(length)
    angle = (index[:, None] * index[None, :] % length).astype(np.float32)
    angle = angle * np.float32(2.0 * math.pi / length)
    factor = np.float32(1.0 / math.sqrt(length))
    cosm = (np.cos(angle) * factor).astype(jnp.bfloat16)
    sinm = (np.sin(angle) * factor).astype(jnp.bfloat16)
    return cosm, sinm


def complex_tables(length, parts):
    cosm, sinm = make_tables(length)
    ahead = np.block([[cosm, sinm], [-sinm, cosm]])
    back = np.block([[cosm, -sinm], [sinm, cosm]])
    block = length // parts
    order = np.arange(2 * length).reshape(2, parts, block).transpose(1, 0, 2).reshape(-1)
    half = length // 2
    zed = np.zeros((2, length, 2, length), np.float32)
    for line in range(2):
        for slot in (0, half):
            zed[line, :, line, slot] = cosm[:, slot]
        slots = slice(line * half + 1, (line + 1) * half)
        zed[line, :, 0, slots] = cosm[:, 1:half]
        zed[line, :, 1, slots] = -sinm[:, 1:half].astype(np.float32)
    dez = 2.0 * zed
    dez[:, :, :, 0] *= 0.5
    dez[:, :, :, half] *= 0.5
    zed = zed.reshape(2 * length, 2 * length).astype(ahead.dtype)
    dez = dez.reshape(2 * length, 2 * length).T.astype(ahead.dtype)
    return (ahead[order], zed), (ahead, back, back[:, order], dez)


def mirror_tables(length):
    half = length // 2
    index = np.arange(length)
    frequency = np.where(index <= half, index, index - half)
    wanted = -frequency % length
    whole = index[:, None] == wanted[None, :]
    low = (index[:, None] < half) & (index[:, None] + half == wanted[None, :])
    high = (index[:, None] >= half) & whole
    flip = index[:, None] == (-index % length)[None, :]
    return np.stack([flip, low, high, whole]).astype(np.float32).astype(jnp.bfloat16)


def dot(left, right):
    return jnp.dot(left, right, preferred_element_type=F32)


def planes_forward(own_ref, other_ref, table_ref, out_ref, held, sems):
    planes, length = own_ref.shape[0], own_ref.shape[1]
    groups = out_ref.shape[0]
    copies = []
    for x in range(0, planes, 2):
        own = own_ref[x : x + 2].astype(F32).reshape(2 * length, length)
        other = other_ref[x : x + 2].astype(F32).reshape(2 * length, length)
        field = jnp.concatenate([(own * own).astype(BF16), (own * other).astype(BF16)], axis=1)
        field = dot(field, table_ref[ZED]).astype(BF16)
        field = jnp.concatenate(
            [
                jnp.concatenate([field[:length, :length], field[length:, :length]], axis=1),
                jnp.concatenate([field[:length, length:], field[length:, length:]], axis=1),
            ],
            axis=0,
        )
        field = dot(table_ref[AHEAD_SORTED], field).astype(BF16)
        held[:, x] = field[:, :length].reshape(groups, -1, length)
        held[:, x + 1] = field[:, length:].reshape(groups, -1, length)
        copies.append(
            pltpu.make_async_copy(held.at[:, x : x + 2], out_ref.at[:, x : x + 2], sems.at[x // 2])
        )
        copies[-1].start()
    for copy in copies:
        copy.wait()


def columns_filter(line_ref, screen_ref, table_ref, out_ref, sent):
    length = line_ref.shape[0]
    columns = line_ref.shape[1] // 2
    lines = jnp.swapaxes(line_ref[...], 0, 1)
    for c in range(0, columns, 2):
        rows = [[part * columns + c + j for j in range(2)] for part in range(2)]
        field = jnp.concatenate(
            [jnp.concatenate([lines[row] for row in pair], axis=1) for pair in rows], axis=0
        )
        field = dot(table_ref[AHEAD], field)
        screen = jnp.concatenate([screen_ref[c], screen_ref[c + 1]], axis=1)
        field = jnp.concatenate([field[:length] * screen, field[length:] * screen], axis=0)
        field = dot(table_ref[BACK], field.astype(BF16)).astype(BF16)
        for part in range(2):
            for j in range(2):
                sent[rows[part][j]] = field[
                    part * length : (part + 1) * length, j * length : (j + 1) * length
                ]
    out_ref[...] = jnp.swapaxes(sent[...], 0, 1)


def planes_back(line_ref, own_ref, other_ref, table_ref, kept_ref, sent_ref):
    planes, length = own_ref.shape[0], own_ref.shape[1]
    for x in range(0, planes, 2):
        field = jnp.concatenate(
            [line_ref[:, x + j].reshape(2 * length, length) for j in range(2)], axis=1
        )
        field = dot(table_ref[BACK_SORTED], field).astype(BF16)
        field = jnp.concatenate(
            [
                jnp.concatenate([field[:length, :length], field[length:, :length]], axis=1),
                jnp.concatenate([field[:length, length:], field[length:, length:]], axis=1),
            ],
            axis=0,
        )
        field = dot(field, table_ref[DEZ])
        own = own_ref[x : x + 2].astype(F32).reshape(2 * length, length)
        other = other_ref[x : x + 2].astype(F32).reshape(2 * length, length)
        kept = field[:, :length] * own + field[:, length:] * other
        sent = (field[:, length:] * own).astype(BF16)
        kept_ref[x : x + 2] = kept.reshape(2, length, length)
        sent_ref[x : x + 2] = sent.reshape(2, length, length)


def relay(there_ref, out_ref):
    out_ref[...] = there_ref[...]


def symmetric_kernel(here_ref, first_ref, second_ref, mirror_ref, out_ref, low, high, zero):
    columns, length = out_ref.shape[0], out_ref.shape[1]
    half = length // 2
    packed = half * columns
    odd = lax.rem(lax.axis_index("band"), 2)

    def spread(main_ref, edge_ref):
        row = lax.broadcasted_iota(jnp.int32, (packed, length), 0)
        for out, choice in ((low, LOW), (high, HIGH)):
            main = dot(main_ref[:packed], mirror_ref[choice])
            edge = dot(edge_ref[:packed], mirror_ref[choice])
            out[...] = jnp.where(lax.rem(row, columns) == 0, edge, main)
        row = lax.broadcasted_iota(jnp.int32, (SPARE, length), 0)
        main, edge = main_ref[packed:].astype(F32), edge_ref[packed:].astype(F32)
        zero[...] = jnp.where(row == 0, edge, main)

    pl.when(odd == 0)(lambda: spread(first_ref, second_ref))
    pl.when(odd == 1)(lambda: spread(second_ref, first_ref))
    zeros = zero[...].astype(BF16)
    slot = lax.broadcasted_iota(jnp.int32, (length, length), 1)
    row = lax.broadcasted_iota(jnp.int32, (SPARE, length), 0)
    first = lax.broadcasted_iota(jnp.int32, (SPARE, length), 1) == 0
    for c in range(columns):
        source = (columns - c) % columns
        other = jnp.concatenate(
            [part[pl.ds(source, half, stride=columns), :] for part in (low, high)], axis=0
        )
        chosen = ((row == source) & first).astype(F32).astype(BF16)
        other = other + lax.dot_general(
            zeros, chosen, (((0,), (0,)), ((), ())), preferred_element_type=F32
        )
        other = dot(mirror_ref[FLIP], other.astype(BF16))
        here = here_ref[pl.ds(c, length, stride=columns), :]
        here = jnp.where(slot <= half, here, pltpu.roll(here, half, 1))
        out_ref[c] = 0.5 * (here + other)


def prepare(first, own_ref, kernel_ref, table_ref, *refs):
    own_out, kernel_out, table_out, packed_out, sems = refs[-5:]

    band = lax.axis_index("band")
    early = (lax.rem(band, 2) == 1) & (band < lax.axis_size("band") - 1)

    @pl.when(early == first)
    def _():
        pairs = (
            (kernel_ref, kernel_out),
            (own_ref, own_out),
            (table_ref, table_out),
        )
        copies = [pltpu.make_async_copy(a, b, sems.at[i]) for i, (a, b) in enumerate(pairs)]
        for copy in copies:
            copy.start()
        copies[0].wait()
        length = kernel_out.shape[1]
        half = length // 2
        columns = kernel_out.shape[0] // length
        packed = half * columns
        lane = lax.broadcasted_iota(jnp.int32, (packed, length), 1)
        packed_out[:packed] = jnp.where(
            lane < half, pltpu.roll(kernel_out[:packed], half, 1), kernel_out[packed:]
        ).astype(BF16)
        row = lax.broadcasted_iota(jnp.int32, (SPARE, length), 0)
        first = lax.broadcasted_iota(jnp.int32, (SPARE, length), 1) == 0
        zeros = jnp.zeros((SPARE, length), F32)
        for c in range(columns):
            plane = kernel_out[pl.ds(c, length, stride=columns), :].astype(BF16)
            chosen = ((row == c) & first).astype(F32).astype(BF16)
            zeros = zeros + lax.dot_general(
                chosen, plane, (((1,), (1,)), ((), ())), preferred_element_type=F32
            )
        packed_out[packed:] = zeros.astype(BF16)
        for copy in copies[1:]:
            copy.wait()


def load(later_ref, table_ref, mirror_ref, table_out, mirror_out, sems):
    pairs = ((table_ref, table_out), (mirror_ref, mirror_out))
    copies = [pltpu.make_async_copy(a, b, sems.at[i]) for i, (a, b) in enumerate(pairs)]
    for copy in copies:
        copy.start()
    for copy in copies:
        copy.wait()


def finish(kept_ref, returned_ref, out_ref, held, sems):
    copies = []
    for i in range(sems.shape[0]):
        part = pl.ds(i * (held.shape[0] // sems.shape[0]), held.shape[0] // sems.shape[0])
        held[part] = kept_ref[part] + returned_ref[part].astype(F32)
        copies.append(pltpu.make_async_copy(held.at[part], out_ref.at[part], sems.at[i]))
        copies[-1].start()
    for copy in copies:
        copy.wait()


def call(body, outs, scratch=(), flops=0, name=None, in_specs=None, out_specs=None, aliases=None,
         limit=VMEM_LIMIT):
    specs = {"in_specs": in_specs, "out_specs": out_specs}
    specs = {key: value for key, value in specs.items() if value is not None}
    return pl.pallas_call(
        body,
        **specs,
        out_shape=outs,
        scratch_shapes=list(scratch),
        input_output_aliases=aliases or {},
        cost_estimate=pl.CostEstimate(flops=flops, bytes_accessed=1 << 20, transcendentals=0),
        compiler_params=pltpu.CompilerParams(vmem_limit_bytes=limit),
        name=name,
    )


def per_device(orbitals, kernel):
    planes, length = orbitals.shape[1], orbitals.shape[2]
    groups = lax.axis_size("fft")
    columns = length // groups
    near, far = (jnp.asarray(np.stack(some)) for some in complex_tables(length, groups))
    mirrors = jnp.asarray(mirror_tables(length))
    work = 8 * planes * length**3

    here = jax.ShapeDtypeStruct((length * columns, length), F32)
    sources = [
        pltpu.with_memory_space_constraint(array, pltpu.HBM)
        for array in (orbitals[0], kernel.reshape(here.shape), near, far, mirrors)
    ]
    results = (
        pltpu.VMEM(orbitals.shape[1:], BF16),
        pltpu.VMEM(here.shape, F32),
        pltpu.VMEM(near.shape, BF16),
        pltpu.VMEM((length // 2 * columns + SPARE, length), BF16),
    )
    anywhere = pl.BlockSpec(memory_space=pl.ANY)
    in_vmem = pl.BlockSpec(memory_space=pltpu.VMEM)
    prepared = call(
        functools.partial(prepare, True),
        results,
        [pltpu.SemaphoreType.DMA((3,))],
        in_specs=[anywhere] * 3,
        limit=NEARLY_ALL,
        name="prepare",
    )(*sources[:3])
    orbitals, *prepared = lax.optimization_barrier((orbitals, *prepared))
    other = from_behind(orbitals[0], "band", 1)
    own, here, near, packed = call(
        functools.partial(prepare, False),
        results,
        [pltpu.SemaphoreType.DMA((3,))],
        in_specs=[anywhere] * 3 + [in_vmem] * 4,
        aliases={3 + i: i for i in range(4)},
        name="prepare",
    )(*sources[:3], *prepared)
    bands = lax.axis_size("band")
    swap = [
        (b * groups + f, b * groups + (groups - 1 - f if b % 2 == 0 else -f % groups))
        for b in range(bands)
        for f in range(groups)
    ]
    there = lax.ppermute(packed, ("band", "fft"), swap)
    relayed = call(
        relay,
        jax.ShapeDtypeStruct(there.shape, BF16),
        flops=100 * 10**9,
        name="relay",
    )(there)
    swapped = from_behind(relayed, "band", -1)
    far, mirrors = call(
        load,
        (jax.ShapeDtypeStruct(far.shape, BF16), jax.ShapeDtypeStruct(mirrors.shape, BF16)),
        [pltpu.SemaphoreType.DMA((2,))],
        in_specs=[anywhere] * 3,
        name="load",
    )(relayed, *sources[3:])

    lines = jax.ShapeDtypeStruct((groups, planes, 2 * columns, length), BF16)
    spectrum = call(
        planes_forward,
        pltpu.HBM(lines.shape, lines.dtype),
        [pltpu.VMEM(lines.shape, BF16), pltpu.SemaphoreType.DMA((planes // 2,))],
        out_specs=pl.BlockSpec(memory_space=pl.ANY),
        name="planes_forward",
    )(
        own, other, near
    )
    spectrum = lax.all_to_all(spectrum, "fft", split_axis=0, concat_axis=0, tiled=True)
    screen = call(
        symmetric_kernel,
        jax.ShapeDtypeStruct((columns, length, length), F32),
        [pltpu.VMEM((length // 2 * columns, length), F32)] * 2
        + [pltpu.VMEM((SPARE, length), F32)],
        flops=work,
        name="symmetric_kernel",
    )(
        here, relayed, swapped, mirrors
    )
    spectrum = call(
        columns_filter,
        jax.ShapeDtypeStruct((length, 2 * columns, length), BF16),
        [pltpu.VMEM((2 * columns, length, length), BF16)],
        flops=2 * work,
        name="columns_filter",
    )(
        spectrum.reshape(length, 2 * columns, length),
        screen,
        far,
    )
    spectrum = spectrum.reshape(groups, planes, 2 * columns, length)
    spectrum = lax.all_to_all(spectrum, "fft", split_axis=0, concat_axis=0, tiled=True)
    kept, sent = call(
        planes_back,
        (
            jax.ShapeDtypeStruct(own.shape, F32),
            jax.ShapeDtypeStruct(own.shape, BF16),
        ),
        flops=2 * work,
        name="planes_back",
    )(spectrum, own, other, far)
    returned = from_behind(sent, "band", -1)
    total = call(
        finish,
        jax.ShapeDtypeStruct(kept.shape, F32),
        [pltpu.VMEM(kept.shape, F32), pltpu.SemaphoreType.DMA((4,))],
        out_specs=pl.BlockSpec(memory_space=pl.ANY),
        name="finish",
    )(kept, returned)
    return total[None]


def solution(mesh):
    in_specs = (P("band", "fft", None, None), P(None, "fft", None))
    out_specs = P("band", "fft", None, None)
    return jax.shard_map(
        per_device, mesh=mesh, in_specs=in_specs, out_specs=out_specs, check_vma=False
    )
```

```python
import functools
import math

import jax
import jax.numpy as jnp
import numpy as np
from jax import lax
from jax.experimental import pallas as pl
from jax.experimental.pallas import tpu as pltpu
from jax.sharding import PartitionSpec as P

F32 = jnp.float32
BF16 = jnp.bfloat16
VMEM_LIMIT = 16 * 1024 * 1024
NEARLY_ALL = 65_700_000
AHEAD_SORTED, ZED = range(2)
AHEAD, BACK, BACK_SORTED, DEZ = range(4)
FLIP, LOW, HIGH, WHOLE = range(4)
SPARE = 16


def from_behind(shard, axis, by):
    devices = lax.axis_size(axis)
    return lax.ppermute(shard, axis, [(i, (i + by) % devices) for i in range(devices)])


def make_tables(length):
    index = np.arange(length)
    angle = (index[:, None] * index[None, :] % length).astype(np.float32)
    angle = angle * np.float32(2.0 * math.pi / length)
    factor = np.float32(1.0 / math.sqrt(length))
    cosm = (np.cos(angle) * factor).astype(jnp.bfloat16)
    sinm = (np.sin(angle) * factor).astype(jnp.bfloat16)
    return cosm, sinm


def complex_tables(length, parts):
    cosm, sinm = make_tables(length)
    ahead = np.block([[cosm, sinm], [-sinm, cosm]])
    back = np.block([[cosm, -sinm], [sinm, cosm]])
    block = length // parts
    order = np.arange(2 * length).reshape(2, parts, block).transpose(1, 0, 2).reshape(-1)
    half = length // 2
    zed = np.zeros((2, length, 2, length), np.float32)
    for line in range(2):
        for slot in (0, half):
            zed[line, :, line, slot] = cosm[:, slot]
        slots = slice(line * half + 1, (line + 1) * half)
        zed[line, :, 0, slots] = cosm[:, 1:half]
        zed[line, :, 1, slots] = -sinm[:, 1:half].astype(np.float32)
    dez = 2.0 * zed
    dez[:, :, :, 0] *= 0.5
    dez[:, :, :, half] *= 0.5
    zed = zed.reshape(2 * length, 2 * length).astype(ahead.dtype)
    dez = dez.reshape(2 * length, 2 * length).T.astype(ahead.dtype)
    return (ahead[order], zed), (ahead, back, back[:, order], dez)


def mirror_tables(length):
    half = length // 2
    index = np.arange(length)
    frequency = np.where(index <= half, index, index - half)
    wanted = -frequency % length
    whole = index[:, None] == wanted[None, :]
    low = (index[:, None] < half) & (index[:, None] + half == wanted[None, :])
    high = (index[:, None] >= half) & whole
    flip = index[:, None] == (-index % length)[None, :]
    return np.stack([flip, low, high, whole]).astype(np.float32).astype(jnp.bfloat16)


def dot(left, right):
    return jnp.dot(left, right, preferred_element_type=F32)


def planes_forward(own_ref, other_ref, table_ref, out_ref, held, sems):
    planes, length = own_ref.shape[0], own_ref.shape[1]
    groups = out_ref.shape[0]
    copies = []
    for x in range(0, planes, 2):
        own = own_ref[x : x + 2].astype(F32).reshape(2 * length, length)
        other = other_ref[x : x + 2].astype(F32).reshape(2 * length, length)
        field = jnp.concatenate([(own * own).astype(BF16), (own * other).astype(BF16)], axis=1)
        field = dot(field, table_ref[ZED]).astype(BF16)
        field = jnp.concatenate(
            [
                jnp.concatenate([field[:length, :length], field[length:, :length]], axis=1),
                jnp.concatenate([field[:length, length:], field[length:, length:]], axis=1),
            ],
            axis=0,
        )
        field = dot(table_ref[AHEAD_SORTED], field).astype(BF16)
        held[:, x] = field[:, :length].reshape(groups, -1, length)
        held[:, x + 1] = field[:, length:].reshape(groups, -1, length)
        copies.append(
            pltpu.make_async_copy(held.at[:, x : x + 2], out_ref.at[:, x : x + 2], sems.at[x // 2])
        )
        copies[-1].start()
    for copy in copies:
        copy.wait()


def columns_filter(line_ref, screen_ref, table_ref, out_ref, sent):
    length = line_ref.shape[0]
    columns = line_ref.shape[1] // 2
    lines = jnp.swapaxes(line_ref[...], 0, 1)
    for c in range(0, columns, 2):
        rows = [[part * columns + c + j for j in range(2)] for part in range(2)]
        field = jnp.concatenate(
            [jnp.concatenate([lines[row] for row in pair], axis=1) for pair in rows], axis=0
        )
        field = dot(table_ref[AHEAD], field)
        screen = jnp.concatenate([screen_ref[c], screen_ref[c + 1]], axis=1)
        field = jnp.concatenate([field[:length] * screen, field[length:] * screen], axis=0)
        field = dot(table_ref[BACK], field.astype(BF16)).astype(BF16)
        for part in range(2):
            for j in range(2):
                sent[rows[part][j]] = field[
                    part * length : (part + 1) * length, j * length : (j + 1) * length
                ]
    out_ref[...] = jnp.swapaxes(sent[...], 0, 1)


def planes_back(line_ref, own_ref, other_ref, table_ref, kept_ref, sent_ref):
    planes, length = own_ref.shape[0], own_ref.shape[1]
    for x in range(0, planes, 2):
        field = jnp.concatenate(
            [line_ref[:, x + j].reshape(2 * length, length) for j in range(2)], axis=1
        )
        field = dot(table_ref[BACK_SORTED], field).astype(BF16)
        field = jnp.concatenate(
            [
                jnp.concatenate([field[:length, :length], field[length:, :length]], axis=1),
                jnp.concatenate([field[:length, length:], field[length:, length:]], axis=1),
            ],
            axis=0,
        )
        field = dot(field, table_ref[DEZ])
        own = own_ref[x : x + 2].astype(F32).reshape(2 * length, length)
        other = other_ref[x : x + 2].astype(F32).reshape(2 * length, length)
        kept = field[:, :length] * own + field[:, length:] * other
        sent = (field[:, length:] * own).astype(BF16)
        kept_ref[x : x + 2] = kept.reshape(2, length, length)
        sent_ref[x : x + 2] = sent.reshape(2, length, length)


def relay(there_ref, out_ref):
    out_ref[...] = there_ref[...]


def symmetric_kernel(here_ref, first_ref, second_ref, mirror_ref, out_ref, low, high, zero):
    columns, length = out_ref.shape[0], out_ref.shape[1]
    half = length // 2
    packed = half * columns
    odd = lax.rem(lax.axis_index("band"), 2)

    def spread(main_ref, edge_ref):
        row = lax.broadcasted_iota(jnp.int32, (packed, length), 0)
        for out, choice in ((low, LOW), (high, HIGH)):
            main = dot(main_ref[:packed], mirror_ref[choice])
            edge = dot(edge_ref[:packed], mirror_ref[choice])
            out[...] = jnp.where(lax.rem(row, columns) == 0, edge, main)
        row = lax.broadcasted_iota(jnp.int32, (SPARE, length), 0)
        main, edge = main_ref[packed:].astype(F32), edge_ref[packed:].astype(F32)
        zero[...] = jnp.where(row == 0, edge, main)

    pl.when(odd == 0)(lambda: spread(first_ref, second_ref))
    pl.when(odd == 1)(lambda: spread(second_ref, first_ref))
    zeros = zero[...].astype(BF16)
    slot = lax.broadcasted_iota(jnp.int32, (length, length), 1)
    row = lax.broadcasted_iota(jnp.int32, (SPARE, length), 0)
    first = lax.broadcasted_iota(jnp.int32, (SPARE, length), 1) == 0
    for c in range(columns):
        source = (columns - c) % columns
        other = jnp.concatenate(
            [part[pl.ds(source, half, stride=columns), :] for part in (low, high)], axis=0
        )
        chosen = ((row == source) & first).astype(F32).astype(BF16)
        other = other + lax.dot_general(
            zeros, chosen, (((0,), (0,)), ((), ())), preferred_element_type=F32
        )
        other = dot(mirror_ref[FLIP], other.astype(BF16))
        here = here_ref[pl.ds(c, length, stride=columns), :]
        here = jnp.where(slot <= half, here, pltpu.roll(here, half, 1))
        out_ref[c] = 0.5 * (here + other)


def prepare(first, own_ref, kernel_ref, table_ref, *refs):
    own_out, kernel_out, table_out, packed_out, sems = refs[-5:]

    band = lax.axis_index("band")
    early = (lax.rem(band, 2) == 1) & (band < lax.axis_size("band") - 1)

    if not first:

        @pl.when(early)
        def _():
            for made, out in zip(refs[:4], refs[4:8]):
                out[...] = made[...]

    @pl.when(early == first)
    def _():
        pairs = (
            (kernel_ref, kernel_out),
            (own_ref, own_out),
            (table_ref, table_out),
        )
        copies = [pltpu.make_async_copy(a, b, sems.at[i]) for i, (a, b) in enumerate(pairs)]
        for copy in copies:
            copy.start()
        copies[0].wait()
        length = kernel_out.shape[1]
        half = length // 2
        columns = kernel_out.shape[0] // length
        packed = half * columns
        lane = lax.broadcasted_iota(jnp.int32, (packed, length), 1)
        packed_out[:packed] = jnp.where(
            lane < half, pltpu.roll(kernel_out[:packed], half, 1), kernel_out[packed:]
        ).astype(BF16)
        row = lax.broadcasted_iota(jnp.int32, (SPARE, length), 0)
        first = lax.broadcasted_iota(jnp.int32, (SPARE, length), 1) == 0
        zeros = jnp.zeros((SPARE, length), F32)
        for c in range(columns):
            plane = kernel_out[pl.ds(c, length, stride=columns), :].astype(BF16)
            chosen = ((row == c) & first).astype(F32).astype(BF16)
            zeros = zeros + lax.dot_general(
                chosen, plane, (((1,), (1,)), ((), ())), preferred_element_type=F32
            )
        packed_out[packed:] = zeros.astype(BF16)
        for copy in copies[1:]:
            copy.wait()


def load(later_ref, table_ref, mirror_ref, table_out, mirror_out, sems):
    pairs = ((table_ref, table_out), (mirror_ref, mirror_out))
    copies = [pltpu.make_async_copy(a, b, sems.at[i]) for i, (a, b) in enumerate(pairs)]
    for copy in copies:
        copy.start()
    for copy in copies:
        copy.wait()


def finish(kept_ref, returned_ref, out_ref, held, sems):
    copies = []
    for i in range(sems.shape[0]):
        part = pl.ds(i * (held.shape[0] // sems.shape[0]), held.shape[0] // sems.shape[0])
        held[part] = kept_ref[part] + returned_ref[part].astype(F32)
        copies.append(pltpu.make_async_copy(held.at[part], out_ref.at[part], sems.at[i]))
        copies[-1].start()
    for copy in copies:
        copy.wait()


def call(body, outs, scratch=(), flops=0, name=None, in_specs=None, out_specs=None, aliases=None,
         limit=VMEM_LIMIT):
    specs = {"in_specs": in_specs, "out_specs": out_specs}
    specs = {key: value for key, value in specs.items() if value is not None}
    return pl.pallas_call(
        body,
        **specs,
        out_shape=outs,
        scratch_shapes=list(scratch),
        input_output_aliases=aliases or {},
        cost_estimate=pl.CostEstimate(flops=flops, bytes_accessed=1 << 20, transcendentals=0),
        compiler_params=pltpu.CompilerParams(vmem_limit_bytes=limit),
        name=name,
    )


def per_device(orbitals, kernel):
    planes, length = orbitals.shape[1], orbitals.shape[2]
    groups = lax.axis_size("fft")
    columns = length // groups
    near, far = (jnp.asarray(np.stack(some)) for some in complex_tables(length, groups))
    mirrors = jnp.asarray(mirror_tables(length))
    work = 8 * planes * length**3

    here = jax.ShapeDtypeStruct((length * columns, length), F32)
    sources = [
        pltpu.with_memory_space_constraint(array, pltpu.HBM)
        for array in (orbitals[0], kernel.reshape(here.shape), near, far, mirrors)
    ]
    results = (
        pltpu.VMEM(orbitals.shape[1:], BF16),
        pltpu.VMEM(here.shape, F32),
        pltpu.VMEM(near.shape, BF16),
        pltpu.VMEM((length // 2 * columns + SPARE, length), BF16),
    )
    anywhere = pl.BlockSpec(memory_space=pl.ANY)
    in_vmem = pl.BlockSpec(memory_space=pltpu.VMEM)
    prepared = call(
        functools.partial(prepare, True),
        results,
        [pltpu.SemaphoreType.DMA((3,))],
        in_specs=[anywhere] * 3,
        limit=NEARLY_ALL,
        name="prepare",
    )(*sources[:3])
    orbitals, *prepared = lax.optimization_barrier((orbitals, *prepared))
    other = from_behind(orbitals[0], "band", 1)
    own, here, near, packed = call(
        functools.partial(prepare, False),
        results,
        [pltpu.SemaphoreType.DMA((3,))],
        in_specs=[anywhere] * 3 + [in_vmem] * 4,
        aliases={3 + i: i for i in range(4)},
        name="prepare",
    )(*sources[:3], *prepared)
    bands = lax.axis_size("band")
    swap = [
        (b * groups + f, b * groups + (groups - 1 - f if b % 2 == 0 else -f % groups))
        for b in range(bands)
        for f in range(groups)
    ]
    there = lax.ppermute(packed, ("band", "fft"), swap)
    relayed = call(
        relay,
        jax.ShapeDtypeStruct(there.shape, BF16),
        flops=100 * 10**9,
        name="relay",
    )(there)
    swapped = from_behind(relayed, "band", -1)
    far, mirrors = call(
        load,
        (jax.ShapeDtypeStruct(far.shape, BF16), jax.ShapeDtypeStruct(mirrors.shape, BF16)),
        [pltpu.SemaphoreType.DMA((2,))],
        in_specs=[anywhere] * 3,
        name="load",
    )(relayed, *sources[3:])

    lines = jax.ShapeDtypeStruct((groups, planes, 2 * columns, length), BF16)
    spectrum = call(
        planes_forward,
        pltpu.HBM(lines.shape, lines.dtype),
        [pltpu.VMEM(lines.shape, BF16), pltpu.SemaphoreType.DMA((planes // 2,))],
        out_specs=pl.BlockSpec(memory_space=pl.ANY),
        name="planes_forward",
    )(
        own, other, near
    )
    spectrum = lax.all_to_all(spectrum, "fft", split_axis=0, concat_axis=0, tiled=True)
    screen = call(
        symmetric_kernel,
        jax.ShapeDtypeStruct((columns, length, length), F32),
        [pltpu.VMEM((length // 2 * columns, length), F32)] * 2
        + [pltpu.VMEM((SPARE, length), F32)],
        flops=work,
        name="symmetric_kernel",
    )(
        here, relayed, swapped, mirrors
    )
    spectrum = call(
        columns_filter,
        jax.ShapeDtypeStruct((length, 2 * columns, length), BF16),
        [pltpu.VMEM((2 * columns, length, length), BF16)],
        flops=2 * work,
        name="columns_filter",
    )(
        spectrum.reshape(length, 2 * columns, length),
        screen,
        far,
    )
    spectrum = spectrum.reshape(groups, planes, 2 * columns, length)
    spectrum = lax.all_to_all(spectrum, "fft", split_axis=0, concat_axis=0, tiled=True)
    kept, sent = call(
        planes_back,
        (
            jax.ShapeDtypeStruct(own.shape, F32),
            jax.ShapeDtypeStruct(own.shape, BF16),
        ),
        flops=2 * work,
        name="planes_back",
    )(spectrum, own, other, far)
    returned = from_behind(sent, "band", -1)
    total = call(
        finish,
        jax.ShapeDtypeStruct(kept.shape, F32),
        [pltpu.VMEM(kept.shape, F32), pltpu.SemaphoreType.DMA((4,))],
        out_specs=pl.BlockSpec(memory_space=pl.ANY),
        name="finish",
    )(kept, returned)
    return total[None]


def solution(mesh):
    in_specs = (P("band", "fft", None, None), P(None, "fft", None))
    out_specs = P("band", "fft", None, None)
    return jax.shard_map(
        per_device, mesh=mesh, in_specs=in_specs, out_specs=out_specs, check_vma=False
    )
```

```python
import functools
import math

import jax
import jax.numpy as jnp
import numpy as np
from jax import lax
from jax.experimental import pallas as pl
from jax.experimental.pallas import tpu as pltpu
from jax.sharding import PartitionSpec as P

F32 = jnp.float32
BF16 = jnp.bfloat16
VMEM_LIMIT = 16 * 1024 * 1024
NEARLY_ALL = 65_700_000
AHEAD_SORTED, ZED = range(2)
AHEAD, BACK, BACK_SORTED, DEZ = range(4)
FLIP, LOW, HIGH, WHOLE = range(4)
SPARE = 16


def from_behind(shard, axis, by):
    devices = lax.axis_size(axis)
    return lax.ppermute(shard, axis, [(i, (i + by) % devices) for i in range(devices)])


def make_tables(length):
    index = np.arange(length)
    angle = (index[:, None] * index[None, :] % length).astype(np.float32)
    angle = angle * np.float32(2.0 * math.pi / length)
    factor = np.float32(1.0 / math.sqrt(length))
    cosm = (np.cos(angle) * factor).astype(jnp.bfloat16)
    sinm = (np.sin(angle) * factor).astype(jnp.bfloat16)
    return cosm, sinm


def complex_tables(length, parts):
    cosm, sinm = make_tables(length)
    ahead = np.block([[cosm, sinm], [-sinm, cosm]])
    back = np.block([[cosm, -sinm], [sinm, cosm]])
    block = length // parts
    order = np.arange(2 * length).reshape(2, parts, block).transpose(1, 0, 2).reshape(-1)
    half = length // 2
    zed = np.zeros((2, length, 2, length), np.float32)
    for line in range(2):
        for slot in (0, half):
            zed[line, :, line, slot] = cosm[:, slot]
        slots = slice(line * half + 1, (line + 1) * half)
        zed[line, :, 0, slots] = cosm[:, 1:half]
        zed[line, :, 1, slots] = -sinm[:, 1:half].astype(np.float32)
    dez = 2.0 * zed
    dez[:, :, :, 0] *= 0.5
    dez[:, :, :, half] *= 0.5
    zed = zed.reshape(2 * length, 2 * length).astype(ahead.dtype)
    dez = dez.reshape(2 * length, 2 * length).T.astype(ahead.dtype)
    return (ahead[order], zed), (ahead, back, back[:, order], dez)


def mirror_tables(length):
    half = length // 2
    index = np.arange(length)
    frequency = np.where(index <= half, index, index - half)
    wanted = -frequency % length
    whole = index[:, None] == wanted[None, :]
    low = (index[:, None] < half) & (index[:, None] + half == wanted[None, :])
    high = (index[:, None] >= half) & whole
    flip = index[:, None] == (-index % length)[None, :]
    return np.stack([flip, low, high, whole]).astype(np.float32).astype(jnp.bfloat16)


def dot(left, right):
    return jnp.dot(left, right, preferred_element_type=F32)


def planes_forward(own_ref, other_ref, table_ref, out_ref, held, sems):
    planes, length = own_ref.shape[0], own_ref.shape[1]
    groups = out_ref.shape[0]
    copies = []
    for x in range(0, planes, 2):
        own = own_ref[x : x + 2].astype(F32).reshape(2 * length, length)
        other = other_ref[x : x + 2].astype(F32).reshape(2 * length, length)
        field = jnp.concatenate([(own * own).astype(BF16), (own * other).astype(BF16)], axis=1)
        field = dot(field, table_ref[ZED]).astype(BF16)
        field = jnp.concatenate(
            [
                jnp.concatenate([field[:length, :length], field[length:, :length]], axis=1),
                jnp.concatenate([field[:length, length:], field[length:, length:]], axis=1),
            ],
            axis=0,
        )
        field = dot(table_ref[AHEAD_SORTED], field).astype(BF16)
        held[:, x] = field[:, :length].reshape(groups, -1, length)
        held[:, x + 1] = field[:, length:].reshape(groups, -1, length)
        copies.append(
            pltpu.make_async_copy(held.at[:, x : x + 2], out_ref.at[:, x : x + 2], sems.at[x // 2])
        )
        copies[-1].start()
    for copy in copies:
        copy.wait()


def columns_filter(line_ref, screen_ref, table_ref, out_ref, sent):
    length = line_ref.shape[0]
    columns = line_ref.shape[1] // 2
    lines = jnp.swapaxes(line_ref[...], 0, 1)
    for c in range(0, columns, 2):
        rows = [[part * columns + c + j for j in range(2)] for part in range(2)]
        field = jnp.concatenate(
            [jnp.concatenate([lines[row] for row in pair], axis=1) for pair in rows], axis=0
        )
        field = dot(table_ref[AHEAD], field)
        screen = jnp.concatenate([screen_ref[c], screen_ref[c + 1]], axis=1)
        field = jnp.concatenate([field[:length] * screen, field[length:] * screen], axis=0)
        field = dot(table_ref[BACK], field.astype(BF16)).astype(BF16)
        for part in range(2):
            for j in range(2):
                sent[rows[part][j]] = field[
                    part * length : (part + 1) * length, j * length : (j + 1) * length
                ]
    out_ref[...] = jnp.swapaxes(sent[...], 0, 1)


def planes_back(line_ref, own_ref, other_ref, table_ref, kept_ref, sent_ref):
    planes, length = own_ref.shape[0], own_ref.shape[1]
    for x in range(0, planes, 2):
        field = jnp.concatenate(
            [line_ref[:, x + j].reshape(2 * length, length) for j in range(2)], axis=1
        )
        field = dot(table_ref[BACK_SORTED], field).astype(BF16)
        field = jnp.concatenate(
            [
                jnp.concatenate([field[:length, :length], field[length:, :length]], axis=1),
                jnp.concatenate([field[:length, length:], field[length:, length:]], axis=1),
            ],
            axis=0,
        )
        field = dot(field, table_ref[DEZ])
        own = own_ref[x : x + 2].astype(F32).reshape(2 * length, length)
        other = other_ref[x : x + 2].astype(F32).reshape(2 * length, length)
        kept = field[:, :length] * own + field[:, length:] * other
        sent = (field[:, length:] * own).astype(BF16)
        kept_ref[x : x + 2] = kept.reshape(2, length, length)
        sent_ref[x : x + 2] = sent.reshape(2, length, length)


def relay(there_ref, out_ref):
    out_ref[...] = there_ref[...]


def symmetric_kernel(here_ref, first_ref, second_ref, mirror_ref, out_ref, low, high, zero):
    columns, length = out_ref.shape[0], out_ref.shape[1]
    half = length // 2
    packed = half * columns
    odd = lax.rem(lax.axis_index("band"), 2)

    def spread(main_ref, edge_ref):
        row = lax.broadcasted_iota(jnp.int32, (packed, length), 0)
        main, edge = main_ref[:packed].astype(F32), edge_ref[:packed].astype(F32)
        block = jnp.where(lax.rem(row, columns) == 0, edge, main).astype(BF16)
        for out, choice in ((low, LOW), (high, HIGH)):
            out[...] = dot(block, mirror_ref[choice])
        row = lax.broadcasted_iota(jnp.int32, (SPARE, length), 0)
        main, edge = main_ref[packed:].astype(F32), edge_ref[packed:].astype(F32)
        zero[...] = jnp.where(row == 0, edge, main)

    pl.when(odd == 0)(lambda: spread(first_ref, second_ref))
    pl.when(odd == 1)(lambda: spread(second_ref, first_ref))
    zeros = zero[...].astype(BF16)
    slot = lax.broadcasted_iota(jnp.int32, (length, length), 1)
    row = lax.broadcasted_iota(jnp.int32, (SPARE, length), 0)
    first = lax.broadcasted_iota(jnp.int32, (SPARE, length), 1) == 0
    for c in range(columns):
        source = (columns - c) % columns
        other = jnp.concatenate(
            [part[pl.ds(source, half, stride=columns), :] for part in (low, high)], axis=0
        )
        chosen = ((row == source) & first).astype(F32).astype(BF16)
        other = other + lax.dot_general(
            zeros, chosen, (((0,), (0,)), ((), ())), preferred_element_type=F32
        )
        other = dot(mirror_ref[FLIP], other.astype(BF16))
        here = here_ref[pl.ds(c, length, stride=columns), :]
        here = jnp.where(slot <= half, here, pltpu.roll(here, half, 1))
        out_ref[c] = 0.5 * (here + other)


def prepare(first, own_ref, kernel_ref, table_ref, *refs):
    own_out, kernel_out, table_out, packed_out, sems = refs[-5:]

    band = lax.axis_index("band")
    early = (lax.rem(band, 2) == 1) & (band < lax.axis_size("band") - 1)

    if not first:

        @pl.when(early)
        def _():
            for made, out in zip(refs[:4], refs[4:8]):
                out[...] = made[...]

    @pl.when(early == first)
    def _():
        pairs = (
            (kernel_ref, kernel_out),
            (own_ref, own_out),
            (table_ref, table_out),
        )
        copies = [pltpu.make_async_copy(a, b, sems.at[i]) for i, (a, b) in enumerate(pairs)]
        for copy in copies:
            copy.start()
        copies[0].wait()
        length = kernel_out.shape[1]
        half = length // 2
        columns = kernel_out.shape[0] // length
        packed = half * columns
        lane = lax.broadcasted_iota(jnp.int32, (packed, length), 1)
        packed_out[:packed] = jnp.where(
            lane < half, pltpu.roll(kernel_out[:packed], half, 1), kernel_out[packed:]
        ).astype(BF16)
        row = lax.broadcasted_iota(jnp.int32, (SPARE, length), 0)
        first = lax.broadcasted_iota(jnp.int32, (SPARE, length), 1) == 0
        zeros = jnp.zeros((SPARE, length), F32)
        for c in range(columns):
            plane = kernel_out[pl.ds(c, length, stride=columns), :].astype(BF16)
            chosen = ((row == c) & first).astype(F32).astype(BF16)
            zeros = zeros + lax.dot_general(
                chosen, plane, (((1,), (1,)), ((), ())), preferred_element_type=F32
            )
        packed_out[packed:] = zeros.astype(BF16)
        for copy in copies[1:]:
            copy.wait()


def load(later_ref, table_ref, mirror_ref, table_out, mirror_out, sems):
    pairs = ((table_ref, table_out), (mirror_ref, mirror_out))
    copies = [pltpu.make_async_copy(a, b, sems.at[i]) for i, (a, b) in enumerate(pairs)]
    for copy in copies:
        copy.start()
    for copy in copies:
        copy.wait()


def finish(kept_ref, returned_ref, out_ref, held, sems):
    copies = []
    for i in range(sems.shape[0]):
        part = pl.ds(i * (held.shape[0] // sems.shape[0]), held.shape[0] // sems.shape[0])
        held[part] = kept_ref[part] + returned_ref[part].astype(F32)
        copies.append(pltpu.make_async_copy(held.at[part], out_ref.at[part], sems.at[i]))
        copies[-1].start()
    for copy in copies:
        copy.wait()


def call(body, outs, scratch=(), flops=0, name=None, in_specs=None, out_specs=None, aliases=None,
         limit=VMEM_LIMIT):
    specs = {"in_specs": in_specs, "out_specs": out_specs}
    specs = {key: value for key, value in specs.items() if value is not None}
    return pl.pallas_call(
        body,
        **specs,
        out_shape=outs,
        scratch_shapes=list(scratch),
        input_output_aliases=aliases or {},
        cost_estimate=pl.CostEstimate(flops=flops, bytes_accessed=1 << 20, transcendentals=0),
        compiler_params=pltpu.CompilerParams(vmem_limit_bytes=limit),
        name=name,
    )


def per_device(orbitals, kernel):
    planes, length = orbitals.shape[1], orbitals.shape[2]
    groups = lax.axis_size("fft")
    columns = length // groups
    near, far = (jnp.asarray(np.stack(some)) for some in complex_tables(length, groups))
    mirrors = jnp.asarray(mirror_tables(length))
    work = 8 * planes * length**3

    here = jax.ShapeDtypeStruct((length * columns, length), F32)
    sources = [
        pltpu.with_memory_space_constraint(array, pltpu.HBM)
        for array in (orbitals[0], kernel.reshape(here.shape), near, far, mirrors)
    ]
    results = (
        pltpu.VMEM(orbitals.shape[1:], BF16),
        pltpu.VMEM(here.shape, F32),
        pltpu.VMEM(near.shape, BF16),
        pltpu.VMEM((length // 2 * columns + SPARE, length), BF16),
    )
    anywhere = pl.BlockSpec(memory_space=pl.ANY)
    in_vmem = pl.BlockSpec(memory_space=pltpu.VMEM)
    prepared = call(
        functools.partial(prepare, True),
        results,
        [pltpu.SemaphoreType.DMA((3,))],
        in_specs=[anywhere] * 3,
        limit=NEARLY_ALL,
        name="prepare",
    )(*sources[:3])
    orbitals, *prepared = lax.optimization_barrier((orbitals, *prepared))
    other = from_behind(orbitals[0], "band", 1)
    own, here, near, packed = call(
        functools.partial(prepare, False),
        results,
        [pltpu.SemaphoreType.DMA((3,))],
        in_specs=[anywhere] * 3 + [in_vmem] * 4,
        aliases={3 + i: i for i in range(4)},
        name="prepare",
    )(*sources[:3], *prepared)
    bands = lax.axis_size("band")
    swap = [
        (b * groups + f, b * groups + (groups - 1 - f if b % 2 == 0 else -f % groups))
        for b in range(bands)
        for f in range(groups)
    ]
    there = lax.ppermute(packed, ("band", "fft"), swap)
    relayed = call(
        relay,
        jax.ShapeDtypeStruct(there.shape, BF16),
        flops=100 * 10**9,
        name="relay",
    )(there)
    swapped = from_behind(relayed, "band", -1)
    far, mirrors = call(
        load,
        (jax.ShapeDtypeStruct(far.shape, BF16), jax.ShapeDtypeStruct(mirrors.shape, BF16)),
        [pltpu.SemaphoreType.DMA((2,))],
        in_specs=[anywhere] * 3,
        name="load",
    )(relayed, *sources[3:])

    lines = jax.ShapeDtypeStruct((groups, planes, 2 * columns, length), BF16)
    spectrum = call(
        planes_forward,
        pltpu.HBM(lines.shape, lines.dtype),
        [pltpu.VMEM(lines.shape, BF16), pltpu.SemaphoreType.DMA((planes // 2,))],
        out_specs=pl.BlockSpec(memory_space=pl.ANY),
        name="planes_forward",
    )(
        own, other, near
    )
    spectrum = lax.all_to_all(spectrum, "fft", split_axis=0, concat_axis=0, tiled=True)
    screen = call(
        symmetric_kernel,
        jax.ShapeDtypeStruct((columns, length, length), F32),
        [pltpu.VMEM((length // 2 * columns, length), F32)] * 2
        + [pltpu.VMEM((SPARE, length), F32)],
        flops=work,
        name="symmetric_kernel",
    )(
        here, relayed, swapped, mirrors
    )
    spectrum = call(
        columns_filter,
        jax.ShapeDtypeStruct((length, 2 * columns, length), BF16),
        [pltpu.VMEM((2 * columns, length, length), BF16)],
        flops=2 * work,
        name="columns_filter",
    )(
        spectrum.reshape(length, 2 * columns, length),
        screen,
        far,
    )
    spectrum = spectrum.reshape(groups, planes, 2 * columns, length)
    spectrum = lax.all_to_all(spectrum, "fft", split_axis=0, concat_axis=0, tiled=True)
    kept, sent = call(
        planes_back,
        (
            jax.ShapeDtypeStruct(own.shape, F32),
            jax.ShapeDtypeStruct(own.shape, BF16),
        ),
        flops=2 * work,
        name="planes_back",
    )(spectrum, own, other, far)
    returned = from_behind(sent, "band", -1)
    total = call(
        finish,
        jax.ShapeDtypeStruct(kept.shape, F32),
        [pltpu.VMEM(kept.shape, F32), pltpu.SemaphoreType.DMA((4,))],
        out_specs=pl.BlockSpec(memory_space=pl.ANY),
        name="finish",
    )(kept, returned)
    return total[None]


def solution(mesh):
    in_specs = (P("band", "fft", None, None), P(None, "fft", None))
    out_specs = P("band", "fft", None, None)
    return jax.shard_map(
        per_device, mesh=mesh, in_specs=in_specs, out_specs=out_specs, check_vma=False
    )
```

```python
import functools
import math

import jax
import jax.numpy as jnp
import numpy as np
from jax import lax
from jax.experimental import pallas as pl
from jax.experimental.pallas import tpu as pltpu
from jax.sharding import PartitionSpec as P

F32 = jnp.float32
BF16 = jnp.bfloat16
VMEM_LIMIT = 16 * 1024 * 1024
NEARLY_ALL = 65_700_000
AHEAD_SORTED, ZED = range(2)
AHEAD, BACK, BACK_SORTED, DEZ = range(4)
FLIP, LOW, HIGH, WHOLE = range(4)
SPARE = 16


def from_behind(shard, axis, by):
    devices = lax.axis_size(axis)
    return lax.ppermute(shard, axis, [(i, (i + by) % devices) for i in range(devices)])


def make_tables(length):
    index = np.arange(length)
    angle = (index[:, None] * index[None, :] % length).astype(np.float32)
    angle = angle * np.float32(2.0 * math.pi / length)
    factor = np.float32(1.0 / math.sqrt(length))
    cosm = (np.cos(angle) * factor).astype(jnp.bfloat16)
    sinm = (np.sin(angle) * factor).astype(jnp.bfloat16)
    return cosm, sinm


def complex_tables(length, parts):
    cosm, sinm = make_tables(length)
    ahead = np.block([[cosm, sinm], [-sinm, cosm]])
    back = np.block([[cosm, -sinm], [sinm, cosm]])
    block = length // parts
    order = np.arange(2 * length).reshape(2, parts, block).transpose(1, 0, 2).reshape(-1)
    half = length // 2
    zed = np.zeros((2, length, 2, length), np.float32)
    for line in range(2):
        for slot in (0, half):
            zed[line, :, line, slot] = cosm[:, slot]
        slots = slice(line * half + 1, (line + 1) * half)
        zed[line, :, 0, slots] = cosm[:, 1:half]
        zed[line, :, 1, slots] = -sinm[:, 1:half].astype(np.float32)
    dez = 2.0 * zed
    dez[:, :, :, 0] *= 0.5
    dez[:, :, :, half] *= 0.5
    zed = zed.reshape(2 * length, 2 * length).astype(ahead.dtype)
    dez = dez.reshape(2 * length, 2 * length).T.astype(ahead.dtype)
    return (ahead[order], zed), (ahead, back, back[:, order], dez)


def mirror_tables(length):
    half = length // 2
    index = np.arange(length)
    frequency = np.where(index <= half, index, index - half)
    wanted = -frequency % length
    whole = index[:, None] == wanted[None, :]
    low = (index[:, None] < half) & (index[:, None] + half == wanted[None, :])
    high = (index[:, None] >= half) & whole
    flip = index[:, None] == (-index % length)[None, :]
    return np.stack([flip, low, high, whole]).astype(np.float32).astype(jnp.bfloat16)


def dot(left, right):
    return jnp.dot(left, right, preferred_element_type=F32)


def planes_forward(own_ref, other_ref, table_ref, out_ref, held, sems):
    planes, length = own_ref.shape[0], own_ref.shape[1]
    groups = out_ref.shape[0]
    copies = []
    for x in range(0, planes, 2):
        own = own_ref[x : x + 2].astype(F32).reshape(2 * length, length)
        other = other_ref[x : x + 2].astype(F32).reshape(2 * length, length)
        field = jnp.concatenate([(own * own).astype(BF16), (own * other).astype(BF16)], axis=1)
        field = dot(field, table_ref[ZED]).astype(BF16)
        field = jnp.concatenate(
            [
                jnp.concatenate([field[:length, :length], field[length:, :length]], axis=1),
                jnp.concatenate([field[:length, length:], field[length:, length:]], axis=1),
            ],
            axis=0,
        )
        field = dot(table_ref[AHEAD_SORTED], field).astype(BF16)
        held[:, x] = field[:, :length].reshape(groups, -1, length)
        held[:, x + 1] = field[:, length:].reshape(groups, -1, length)
        copies.append(
            pltpu.make_async_copy(held.at[:, x : x + 2], out_ref.at[:, x : x + 2], sems.at[x // 2])
        )
        copies[-1].start()
    for copy in copies:
        copy.wait()


def columns_filter(line_ref, screen_ref, table_ref, out_ref, sent):
    length = line_ref.shape[0]
    columns = line_ref.shape[1] // 2
    lines = jnp.swapaxes(line_ref[...], 0, 1)
    for c in range(0, columns, 2):
        rows = [[part * columns + c + j for j in range(2)] for part in range(2)]
        field = jnp.concatenate(
            [jnp.concatenate([lines[row] for row in pair], axis=1) for pair in rows], axis=0
        )
        field = dot(table_ref[AHEAD], field)
        screen = jnp.concatenate([screen_ref[c], screen_ref[c + 1]], axis=1)
        field = jnp.concatenate([field[:length] * screen, field[length:] * screen], axis=0)
        field = dot(table_ref[BACK], field.astype(BF16)).astype(BF16)
        for part in range(2):
            for j in range(2):
                sent[rows[part][j]] = field[
                    part * length : (part + 1) * length, j * length : (j + 1) * length
                ]
    out_ref[...] = jnp.swapaxes(sent[...], 0, 1)


def planes_back(line_ref, own_ref, other_ref, table_ref, kept_ref, sent_ref):
    planes, length = own_ref.shape[0], own_ref.shape[1]
    for x in range(0, planes, 2):
        field = jnp.concatenate(
            [line_ref[:, x + j].reshape(2 * length, length) for j in range(2)], axis=1
        )
        field = dot(table_ref[BACK_SORTED], field).astype(BF16)
        field = jnp.concatenate(
            [
                jnp.concatenate([field[:length, :length], field[length:, :length]], axis=1),
                jnp.concatenate([field[:length, length:], field[length:, length:]], axis=1),
            ],
            axis=0,
        )
        field = dot(field, table_ref[DEZ])
        own = own_ref[x : x + 2].astype(F32).reshape(2 * length, length)
        other = other_ref[x : x + 2].astype(F32).reshape(2 * length, length)
        kept = field[:, :length] * own + field[:, length:] * other
        sent = (field[:, length:] * own).astype(BF16)
        kept_ref[x : x + 2] = kept.reshape(2, length, length)
        sent_ref[x : x + 2] = sent.reshape(2, length, length)


def relay(there_ref, out_ref):
    out_ref[...] = there_ref[...]


def symmetric_kernel(here_ref, first_ref, second_ref, mirror_ref, out_ref, low, high, zero):
    columns, length = out_ref.shape[0], out_ref.shape[1]
    half = length // 2
    packed = half * columns
    odd = lax.rem(lax.axis_index("band"), 2)

    def spread(main_ref, edge_ref):
        row = lax.broadcasted_iota(jnp.int32, (packed, length), 0)
        main, edge = main_ref[:packed].astype(F32), edge_ref[:packed].astype(F32)
        block = jnp.where(lax.rem(row, columns) == 0, edge, main).astype(BF16)
        for out, choice in ((low, LOW), (high, HIGH)):
            out[...] = dot(block, mirror_ref[choice])
        lane = lax.broadcasted_iota(jnp.int32, (SPARE, length), 1)
        main, edge = main_ref[packed:].astype(F32), edge_ref[packed:].astype(F32)
        zero[...] = jnp.where(lax.rem(lane, columns) == 0, edge, main)

    pl.when(odd == 0)(lambda: spread(first_ref, second_ref))
    pl.when(odd == 1)(lambda: spread(second_ref, first_ref))
    slot = lax.broadcasted_iota(jnp.int32, (length, length), 1)
    plane = lax.broadcasted_iota(jnp.int32, (length, length), 0)
    share = length // columns
    pick = lax.broadcasted_iota(jnp.int32, (length, SPARE), 1)
    pick = lax.broadcasted_iota(jnp.int32, (length, SPARE), 0) // share == pick
    zeros = dot(pick.astype(F32).astype(BF16), zero[...].astype(BF16))
    for c in range(columns):
        source = (columns - c) % columns
        other = jnp.concatenate(
            [part[pl.ds(source, half, stride=columns), :] for part in (low, high)], axis=0
        )
        chosen = jnp.where(slot == plane % share * columns + source, zeros, 0.0)
        chosen = jnp.sum(chosen, axis=1, keepdims=True)
        other = other + jnp.where(slot == 0, chosen, 0.0)
        other = dot(mirror_ref[FLIP], other.astype(BF16))
        here = here_ref[pl.ds(c, length, stride=columns), :]
        here = jnp.where(slot <= half, here, pltpu.roll(here, half, 1))
        out_ref[c] = 0.5 * (here + other)


def prepare(first, own_ref, kernel_ref, table_ref, *refs):
    own_out, kernel_out, table_out, packed_out, sems = refs[-5:]
    band = lax.axis_index("band")
    early = (lax.rem(band, 2) == 1) & (band < lax.axis_size("band") - 1)

    if not first:

        @pl.when(early)
        def _():
            for made, out in zip(refs[:4], refs[4:8]):
                out[...] = made[...]

    @pl.when(early == first)
    def _():
        pairs = ((kernel_ref, kernel_out), (own_ref, own_out), (table_ref, table_out))
        copies = [pltpu.make_async_copy(a, b, sems.at[i]) for i, (a, b) in enumerate(pairs)]
        for copy in copies:
            copy.start()
        copies[0].wait()
        length = kernel_out.shape[1]
        half = length // 2
        columns = kernel_out.shape[0] // length
        packed = half * columns
        lane = lax.broadcasted_iota(jnp.int32, (packed, length), 1)
        packed_out[:packed] = jnp.where(
            lane < half, pltpu.roll(kernel_out[:packed], half, 1), kernel_out[packed:]
        ).astype(BF16)
        row = lax.broadcasted_iota(jnp.int32, (SPARE, length), 0)
        lowest = lax.broadcasted_iota(jnp.int32, (SPARE, length), 1) == 0
        line = lax.dot_general(
            lowest.astype(F32).astype(BF16),
            kernel_out[...].astype(BF16),
            (((1,), (1,)), ((), ())),
            preferred_element_type=F32,
        )
        zeros = jnp.zeros((SPARE, length), F32)
        for j in range(columns):
            zeros = jnp.where(row == j, line[:, j * length : (j + 1) * length], zeros)
        packed_out[packed:] = zeros.astype(BF16)
        for copy in copies[1:]:
            copy.wait()


def load(later_ref, table_ref, mirror_ref, table_out, mirror_out, sems):
    pairs = ((table_ref, table_out), (mirror_ref, mirror_out))
    copies = [pltpu.make_async_copy(a, b, sems.at[i]) for i, (a, b) in enumerate(pairs)]
    for copy in copies:
        copy.start()
    for copy in copies:
        copy.wait()


def finish(kept_ref, returned_ref, out_ref, held, sems):
    copies = []
    for i in range(sems.shape[0]):
        part = pl.ds(i * (held.shape[0] // sems.shape[0]), held.shape[0] // sems.shape[0])
        held[part] = kept_ref[part] + returned_ref[part].astype(F32)
        copies.append(pltpu.make_async_copy(held.at[part], out_ref.at[part], sems.at[i]))
        copies[-1].start()
    for copy in copies:
        copy.wait()


def call(body, outs, scratch=(), flops=0, name=None, in_specs=None, out_specs=None, aliases=None,
         limit=VMEM_LIMIT):
    specs = {"in_specs": in_specs, "out_specs": out_specs}
    specs = {key: value for key, value in specs.items() if value is not None}
    return pl.pallas_call(
        body,
        **specs,
        out_shape=outs,
        scratch_shapes=list(scratch),
        input_output_aliases=aliases or {},
        cost_estimate=pl.CostEstimate(flops=flops, bytes_accessed=1 << 20, transcendentals=0),
        compiler_params=pltpu.CompilerParams(vmem_limit_bytes=limit),
        name=name,
    )


def per_device(orbitals, kernel):
    planes, length = orbitals.shape[1], orbitals.shape[2]
    groups = lax.axis_size("fft")
    columns = length // groups
    near, far = (jnp.asarray(np.stack(some)) for some in complex_tables(length, groups))
    mirrors = jnp.asarray(mirror_tables(length))
    work = 8 * planes * length**3

    here = jax.ShapeDtypeStruct((length * columns, length), F32)
    sources = [
        pltpu.with_memory_space_constraint(array, pltpu.HBM)
        for array in (orbitals[0], kernel.reshape(here.shape), near, far, mirrors)
    ]
    results = (
        pltpu.VMEM(orbitals.shape[1:], BF16),
        pltpu.VMEM(here.shape, F32),
        pltpu.VMEM(near.shape, BF16),
        pltpu.VMEM((length // 2 * columns + SPARE, length), BF16),
    )
    anywhere = pl.BlockSpec(memory_space=pl.ANY)
    in_vmem = pl.BlockSpec(memory_space=pltpu.VMEM)
    prepared = call(
        functools.partial(prepare, True),
        results,
        [pltpu.SemaphoreType.DMA((3,))],
        in_specs=[anywhere] * 3,
        limit=NEARLY_ALL,
        name="prepare",
    )(*sources[:3])
    orbitals, *prepared = lax.optimization_barrier((orbitals, *prepared))
    other = from_behind(orbitals[0], "band", 1)
    own, here, near, packed = call(
        functools.partial(prepare, False),
        results,
        [pltpu.SemaphoreType.DMA((3,))],
        in_specs=[anywhere] * 3 + [in_vmem] * 4,
        aliases={3 + i: i for i in range(4)},
        name="prepare",
    )(*sources[:3], *prepared)
    bands = lax.axis_size("band")
    swap = [
        (b * groups + f, b * groups + (groups - 1 - f if b % 2 == 0 else -f % groups))
        for b in range(bands)
        for f in range(groups)
    ]
    there = lax.ppermute(packed, ("band", "fft"), swap)
    relayed = call(
        relay,
        jax.ShapeDtypeStruct(there.shape, BF16),
        flops=100 * 10**9,
        name="relay",
    )(there)
    swapped = from_behind(relayed, "band", -1)
    far, mirrors = call(
        load,
        (jax.ShapeDtypeStruct(far.shape, BF16), jax.ShapeDtypeStruct(mirrors.shape, BF16)),
        [pltpu.SemaphoreType.DMA((2,))],
        in_specs=[anywhere] * 3,
        name="load",
    )(relayed, *sources[3:])

    lines = jax.ShapeDtypeStruct((groups, planes, 2 * columns, length), BF16)
    spectrum = call(
        planes_forward,
        pltpu.HBM(lines.shape, lines.dtype),
        [pltpu.VMEM(lines.shape, BF16), pltpu.SemaphoreType.DMA((planes // 2,))],
        out_specs=pl.BlockSpec(memory_space=pl.ANY),
        name="planes_forward",
    )(
        own, other, near
    )
    spectrum = lax.all_to_all(spectrum, "fft", split_axis=0, concat_axis=0, tiled=True)
    screen = call(
        symmetric_kernel,
        jax.ShapeDtypeStruct((columns, length, length), F32),
        [pltpu.VMEM((length // 2 * columns, length), F32)] * 2
        + [pltpu.VMEM((SPARE, length), F32)],
        flops=work,
        name="symmetric_kernel",
    )(
        here, relayed, swapped, mirrors
    )
    spectrum = call(
        columns_filter,
        jax.ShapeDtypeStruct((length, 2 * columns, length), BF16),
        [pltpu.VMEM((2 * columns, length, length), BF16)],
        flops=2 * work,
        name="columns_filter",
    )(
        spectrum.reshape(length, 2 * columns, length),
        screen,
        far,
    )
    spectrum = spectrum.reshape(groups, planes, 2 * columns, length)
    spectrum = lax.all_to_all(spectrum, "fft", split_axis=0, concat_axis=0, tiled=True)
    kept, sent = call(
        planes_back,
        (
            jax.ShapeDtypeStruct(own.shape, F32),
            jax.ShapeDtypeStruct(own.shape, BF16),
        ),
        flops=2 * work,
        name="planes_back",
    )(spectrum, own, other, far)
    returned = from_behind(sent, "band", -1)
    total = call(
        finish,
        jax.ShapeDtypeStruct(kept.shape, F32),
        [pltpu.VMEM(kept.shape, F32), pltpu.SemaphoreType.DMA((4,))],
        out_specs=pl.BlockSpec(memory_space=pl.ANY),
        name="finish",
    )(kept, returned)
    return total[None]


def solution(mesh):
    in_specs = (P("band", "fft", None, None), P(None, "fft", None))
    out_specs = P("band", "fft", None, None)
    return jax.shard_map(
        per_device, mesh=mesh, in_specs=in_specs, out_specs=out_specs, check_vma=False
    )
```

```python
import functools
import math

import jax
import jax.numpy as jnp
import numpy as np
from jax import lax
from jax.experimental import pallas as pl
from jax.experimental.pallas import tpu as pltpu
from jax.sharding import PartitionSpec as P

F32 = jnp.float32
BF16 = jnp.bfloat16
VMEM_LIMIT = 16 * 1024 * 1024
NEARLY_ALL = 65_700_000
AHEAD_SORTED, ZED = range(2)
AHEAD, BACK, BACK_SORTED, DEZ = range(4)
FLIP, LOW, HIGH, WHOLE = range(4)
SPARE = 16


def from_behind(shard, axis, by):
    devices = lax.axis_size(axis)
    return lax.ppermute(shard, axis, [(i, (i + by) % devices) for i in range(devices)])


def make_tables(length):
    index = np.arange(length)
    angle = (index[:, None] * index[None, :] % length).astype(np.float32)
    angle = angle * np.float32(2.0 * math.pi / length)
    factor = np.float32(1.0 / math.sqrt(length))
    cosm = (np.cos(angle) * factor).astype(jnp.bfloat16)
    sinm = (np.sin(angle) * factor).astype(jnp.bfloat16)
    return cosm, sinm


def complex_tables(length, parts):
    cosm, sinm = make_tables(length)
    ahead = np.block([[cosm, sinm], [-sinm, cosm]])
    back = np.block([[cosm, -sinm], [sinm, cosm]])
    block = length // parts
    order = np.arange(2 * length).reshape(2, parts, block).transpose(1, 0, 2).reshape(-1)
    half = length // 2
    zed = np.zeros((2, length, 2, length), np.float32)
    for line in range(2):
        for slot in (0, half):
            zed[line, :, line, slot] = cosm[:, slot]
        slots = slice(line * half + 1, (line + 1) * half)
        zed[line, :, 0, slots] = cosm[:, 1:half]
        zed[line, :, 1, slots] = -sinm[:, 1:half].astype(np.float32)
    dez = 2.0 * zed
    dez[:, :, :, 0] *= 0.5
    dez[:, :, :, half] *= 0.5
    zed = zed.reshape(2 * length, 2 * length).astype(ahead.dtype)
    dez = dez.reshape(2 * length, 2 * length).T.astype(ahead.dtype)
    return (ahead[order], zed), (ahead, back, back[:, order], dez)


def mirror_tables(length):
    half = length // 2
    index = np.arange(length)
    frequency = np.where(index <= half, index, index - half)
    wanted = -frequency % length
    whole = index[:, None] == wanted[None, :]
    low = (index[:, None] < half) & (index[:, None] + half == wanted[None, :])
    high = (index[:, None] >= half) & whole
    flip = index[:, None] == (-index % length)[None, :]
    return np.stack([flip, low, high, whole]).astype(np.float32).astype(jnp.bfloat16)


def dot(left, right):
    return jnp.dot(left, right, preferred_element_type=F32)


def planes_forward(own_ref, other_ref, table_ref, out_ref, held, sems):
    planes, length = own_ref.shape[0], own_ref.shape[1]
    groups = out_ref.shape[0]
    copies = []
    for x in range(0, planes, 2):
        own = own_ref[x : x + 2].astype(F32).reshape(2 * length, length)
        other = other_ref[x : x + 2].astype(F32).reshape(2 * length, length)
        field = jnp.concatenate([(own * own).astype(BF16), (own * other).astype(BF16)], axis=1)
        field = dot(field, table_ref[ZED]).astype(BF16)
        field = jnp.concatenate(
            [
                jnp.concatenate([field[:length, :length], field[length:, :length]], axis=1),
                jnp.concatenate([field[:length, length:], field[length:, length:]], axis=1),
            ],
            axis=0,
        )
        field = dot(table_ref[AHEAD_SORTED], field).astype(BF16)
        held[:, x] = field[:, :length].reshape(groups, -1, length)
        held[:, x + 1] = field[:, length:].reshape(groups, -1, length)
        copies.append(
            pltpu.make_async_copy(held.at[:, x : x + 2], out_ref.at[:, x : x + 2], sems.at[x // 2])
        )
        copies[-1].start()
    for copy in copies:
        copy.wait()


def columns_filter(line_ref, screen_ref, table_ref, out_ref, sent):
    length = line_ref.shape[0]
    columns = line_ref.shape[1] // 2
    lines = jnp.swapaxes(line_ref[...], 0, 1)
    for c in range(0, columns, 2):
        rows = [[part * columns + c + j for j in range(2)] for part in range(2)]
        field = jnp.concatenate(
            [jnp.concatenate([lines[row] for row in pair], axis=1) for pair in rows], axis=0
        )
        field = dot(table_ref[AHEAD], field)
        screen = jnp.concatenate([screen_ref[c], screen_ref[c + 1]], axis=1)
        field = jnp.concatenate([field[:length] * screen, field[length:] * screen], axis=0)
        field = dot(table_ref[BACK], field.astype(BF16)).astype(BF16)
        for part in range(2):
            for j in range(2):
                sent[rows[part][j]] = field[
                    part * length : (part + 1) * length, j * length : (j + 1) * length
                ]
    out_ref[...] = jnp.swapaxes(sent[...], 0, 1)


def back_along_y(line_ref, table_ref, x):
    length = line_ref.shape[3]
    field = jnp.concatenate(
        [line_ref[:, x + j].reshape(2 * length, length) for j in range(2)], axis=1
    )
    field = dot(table_ref[BACK_SORTED], field).astype(BF16)
    return jnp.concatenate(
        [
            jnp.concatenate([field[:length, :length], field[length:, :length]], axis=1),
            jnp.concatenate([field[:length, length:], field[length:, length:]], axis=1),
        ],
        axis=0,
    )


def planes_sent(line_ref, own_ref, table_ref, sent_ref):
    planes, length = own_ref.shape[0], own_ref.shape[1]
    for x in range(0, planes, 2):
        field = back_along_y(line_ref, table_ref, x)
        field = dot(field, table_ref[DEZ])[:, length:]
        own = own_ref[x : x + 2].astype(F32).reshape(2 * length, length)
        sent_ref[x : x + 2] = (field * own).astype(BF16).reshape(2, length, length)


def planes_kept(line_ref, own_ref, other_ref, table_ref, kept_ref):
    planes, length = own_ref.shape[0], own_ref.shape[1]
    for x in range(0, planes, 2):
        field = dot(back_along_y(line_ref, table_ref, x), table_ref[DEZ])
        own = own_ref[x : x + 2].astype(F32).reshape(2 * length, length)
        other = other_ref[x : x + 2].astype(F32).reshape(2 * length, length)
        kept = field[:, :length] * own + field[:, length:] * other
        kept_ref[x : x + 2] = kept.reshape(2, length, length)


def relay(there_ref, out_ref):
    out_ref[...] = there_ref[...]


def symmetric_kernel(here_ref, first_ref, second_ref, mirror_ref, out_ref, low, high, zero):
    columns, length = out_ref.shape[0], out_ref.shape[1]
    half = length // 2
    packed = half * columns
    odd = lax.rem(lax.axis_index("band"), 2)

    def spread(main_ref, edge_ref):
        row = lax.broadcasted_iota(jnp.int32, (packed, length), 0)
        for out, choice in ((low, LOW), (high, HIGH)):
            main = dot(main_ref[:packed], mirror_ref[choice])
            edge = dot(edge_ref[:packed], mirror_ref[choice])
            out[...] = jnp.where(lax.rem(row, columns) == 0, edge, main)
        row = lax.broadcasted_iota(jnp.int32, (SPARE, length), 0)
        main, edge = main_ref[packed:].astype(F32), edge_ref[packed:].astype(F32)
        zero[...] = jnp.where(row == 0, edge, main)

    pl.when(odd == 0)(lambda: spread(first_ref, second_ref))
    pl.when(odd == 1)(lambda: spread(second_ref, first_ref))
    zeros = zero[...].astype(BF16)
    slot = lax.broadcasted_iota(jnp.int32, (length, length), 1)
    row = lax.broadcasted_iota(jnp.int32, (SPARE, length), 0)
    first = lax.broadcasted_iota(jnp.int32, (SPARE, length), 1) == 0
    for c in range(columns):
        source = (columns - c) % columns
        other = jnp.concatenate(
            [part[pl.ds(source, half, stride=columns), :] for part in (low, high)], axis=0
        )
        chosen = ((row == source) & first).astype(F32).astype(BF16)
        other = other + lax.dot_general(
            zeros, chosen, (((0,), (0,)), ((), ())), preferred_element_type=F32
        )
        other = dot(mirror_ref[FLIP], other.astype(BF16))
        here = here_ref[pl.ds(c, length, stride=columns), :]
        here = jnp.where(slot <= half, here, pltpu.roll(here, half, 1))
        out_ref[c] = 0.5 * (here + other)


def prepare(first, own_ref, kernel_ref, table_ref, *refs):
    own_out, kernel_out, table_out, packed_out, sems = refs[-5:]

    band = lax.axis_index("band")
    early = (lax.rem(band, 2) == 1) & (band < lax.axis_size("band") - 1)

    if not first:

        @pl.when(early)
        def _():
            for made, out in zip(refs[:4], refs[4:8]):
                out[...] = made[...]

    @pl.when(early == first)
    def _():
        pairs = (
            (kernel_ref, kernel_out),
            (own_ref, own_out),
            (table_ref, table_out),
        )
        copies = [pltpu.make_async_copy(a, b, sems.at[i]) for i, (a, b) in enumerate(pairs)]
        for copy in copies:
            copy.start()
        copies[0].wait()
        length = kernel_out.shape[1]
        half = length // 2
        columns = kernel_out.shape[0] // length
        packed = half * columns
        lane = lax.broadcasted_iota(jnp.int32, (packed, length), 1)
        packed_out[:packed] = jnp.where(
            lane < half, pltpu.roll(kernel_out[:packed], half, 1), kernel_out[packed:]
        ).astype(BF16)
        row = lax.broadcasted_iota(jnp.int32, (SPARE, length), 0)
        first = lax.broadcasted_iota(jnp.int32, (SPARE, length), 1) == 0
        zeros = jnp.zeros((SPARE, length), F32)
        for c in range(columns):
            plane = kernel_out[pl.ds(c, length, stride=columns), :].astype(BF16)
            chosen = ((row == c) & first).astype(F32).astype(BF16)
            zeros = zeros + lax.dot_general(
                chosen, plane, (((1,), (1,)), ((), ())), preferred_element_type=F32
            )
        packed_out[packed:] = zeros.astype(BF16)
        for copy in copies[1:]:
            copy.wait()


def load(later_ref, table_ref, mirror_ref, table_out, mirror_out, sems):
    pairs = ((table_ref, table_out), (mirror_ref, mirror_out))
    copies = [pltpu.make_async_copy(a, b, sems.at[i]) for i, (a, b) in enumerate(pairs)]
    for copy in copies:
        copy.start()
    for copy in copies:
        copy.wait()


def finish(kept_ref, returned_ref, out_ref, held, sems):
    copies = []
    for i in range(sems.shape[0]):
        part = pl.ds(i * (held.shape[0] // sems.shape[0]), held.shape[0] // sems.shape[0])
        held[part] = kept_ref[part] + returned_ref[part].astype(F32)
        copies.append(pltpu.make_async_copy(held.at[part], out_ref.at[part], sems.at[i]))
        copies[-1].start()
    for copy in copies:
        copy.wait()


def call(body, outs, scratch=(), flops=0, name=None, in_specs=None, out_specs=None, aliases=None,
         limit=VMEM_LIMIT):
    specs = {"in_specs": in_specs, "out_specs": out_specs}
    specs = {key: value for key, value in specs.items() if value is not None}
    return pl.pallas_call(
        body,
        **specs,
        out_shape=outs,
        scratch_shapes=list(scratch),
        input_output_aliases=aliases or {},
        cost_estimate=pl.CostEstimate(flops=flops, bytes_accessed=1 << 20, transcendentals=0),
        compiler_params=pltpu.CompilerParams(vmem_limit_bytes=limit),
        name=name,
    )


def per_device(orbitals, kernel):
    planes, length = orbitals.shape[1], orbitals.shape[2]
    groups = lax.axis_size("fft")
    columns = length // groups
    near, far = (jnp.asarray(np.stack(some)) for some in complex_tables(length, groups))
    mirrors = jnp.asarray(mirror_tables(length))
    work = 8 * planes * length**3

    here = jax.ShapeDtypeStruct((length * columns, length), F32)
    sources = [
        pltpu.with_memory_space_constraint(array, pltpu.HBM)
        for array in (orbitals[0], kernel.reshape(here.shape), near, far, mirrors)
    ]
    results = (
        pltpu.VMEM(orbitals.shape[1:], BF16),
        pltpu.VMEM(here.shape, F32),
        pltpu.VMEM(near.shape, BF16),
        pltpu.VMEM((length // 2 * columns + SPARE, length), BF16),
    )
    anywhere = pl.BlockSpec(memory_space=pl.ANY)
    in_vmem = pl.BlockSpec(memory_space=pltpu.VMEM)
    prepared = call(
        functools.partial(prepare, True),
        results,
        [pltpu.SemaphoreType.DMA((3,))],
        in_specs=[anywhere] * 3,
        limit=NEARLY_ALL,
        name="prepare",
    )(*sources[:3])
    orbitals, *prepared = lax.optimization_barrier((orbitals, *prepared))
    other = from_behind(orbitals[0], "band", 1)
    own, here, near, packed = call(
        functools.partial(prepare, False),
        results,
        [pltpu.SemaphoreType.DMA((3,))],
        in_specs=[anywhere] * 3 + [in_vmem] * 4,
        aliases={3 + i: i for i in range(4)},
        name="prepare",
    )(*sources[:3], *prepared)
    bands = lax.axis_size("band")
    swap = [
        (b * groups + f, b * groups + (groups - 1 - f if b % 2 == 0 else -f % groups))
        for b in range(bands)
        for f in range(groups)
    ]
    there = lax.ppermute(packed, ("band", "fft"), swap)
    relayed = call(
        relay,
        jax.ShapeDtypeStruct(there.shape, BF16),
        flops=100 * 10**9,
        name="relay",
    )(there)
    swapped = from_behind(relayed, "band", -1)
    far, mirrors = call(
        load,
        (jax.ShapeDtypeStruct(far.shape, BF16), jax.ShapeDtypeStruct(mirrors.shape, BF16)),
        [pltpu.SemaphoreType.DMA((2,))],
        in_specs=[anywhere] * 3,
        name="load",
    )(relayed, *sources[3:])

    lines = jax.ShapeDtypeStruct((groups, planes, 2 * columns, length), BF16)
    spectrum = call(
        planes_forward,
        pltpu.HBM(lines.shape, lines.dtype),
        [pltpu.VMEM(lines.shape, BF16), pltpu.SemaphoreType.DMA((planes // 2,))],
        out_specs=pl.BlockSpec(memory_space=pl.ANY),
        name="planes_forward",
    )(
        own, other, near
    )
    spectrum = lax.all_to_all(spectrum, "fft", split_axis=0, concat_axis=0, tiled=True)
    screen = call(
        symmetric_kernel,
        jax.ShapeDtypeStruct((columns, length, length), F32),
        [pltpu.VMEM((length // 2 * columns, length), F32)] * 2
        + [pltpu.VMEM((SPARE, length), F32)],
        flops=work,
        name="symmetric_kernel",
    )(
        here, relayed, swapped, mirrors
    )
    spectrum = call(
        columns_filter,
        jax.ShapeDtypeStruct((length, 2 * columns, length), BF16),
        [pltpu.VMEM((2 * columns, length, length), BF16)],
        flops=2 * work,
        name="columns_filter",
    )(
        spectrum.reshape(length, 2 * columns, length),
        screen,
        far,
    )
    spectrum = spectrum.reshape(groups, planes, 2 * columns, length)
    spectrum = lax.all_to_all(spectrum, "fft", split_axis=0, concat_axis=0, tiled=True)
    sent = call(
        planes_sent,
        jax.ShapeDtypeStruct(own.shape, BF16),
        flops=work,
        name="planes_sent",
    )(spectrum, own, far)
    returned = from_behind(sent, "band", -1)
    kept = call(
        planes_kept,
        jax.ShapeDtypeStruct(own.shape, F32),
        flops=2 * work,
        name="planes_kept",
    )(spectrum, own, other, far)
    total = call(
        finish,
        jax.ShapeDtypeStruct(kept.shape, F32),
        [pltpu.VMEM(kept.shape, F32), pltpu.SemaphoreType.DMA((4,))],
        out_specs=pl.BlockSpec(memory_space=pl.ANY),
        name="finish",
    )(kept, returned)
    return total[None]


def solution(mesh):
    in_specs = (P("band", "fft", None, None), P(None, "fft", None))
    out_specs = P("band", "fft", None, None)
    return jax.shard_map(
        per_device, mesh=mesh, in_specs=in_specs, out_specs=out_specs, check_vma=False
    )
```

```python
import functools
import math

import jax
import jax.numpy as jnp
import numpy as np
from jax import lax
from jax.experimental import pallas as pl
from jax.experimental.pallas import tpu as pltpu
from jax.sharding import PartitionSpec as P

F32 = jnp.float32
BF16 = jnp.bfloat16
VMEM_LIMIT = 16 * 1024 * 1024
NEARLY_ALL = 65_700_000
AHEAD_SORTED, ZED = range(2)
AHEAD, BACK, BACK_SORTED, DEZ = range(4)
FLIP, LOW, HIGH, WHOLE = range(4)
SPARE = 16


def from_behind(shard, axis, by):
    devices = lax.axis_size(axis)
    return lax.ppermute(shard, axis, [(i, (i + by) % devices) for i in range(devices)])


def make_tables(length):
    index = np.arange(length)
    angle = (index[:, None] * index[None, :] % length).astype(np.float32)
    angle = angle * np.float32(2.0 * math.pi / length)
    factor = np.float32(1.0 / math.sqrt(length))
    cosm = (np.cos(angle) * factor).astype(jnp.bfloat16)
    sinm = (np.sin(angle) * factor).astype(jnp.bfloat16)
    return cosm, sinm


def complex_tables(length, parts):
    cosm, sinm = make_tables(length)
    ahead = np.block([[cosm, sinm], [-sinm, cosm]])
    back = np.block([[cosm, -sinm], [sinm, cosm]])
    block = length // parts
    order = np.arange(2 * length).reshape(2, parts, block).transpose(1, 0, 2).reshape(-1)
    half = length // 2
    zed = np.zeros((2, length, 2, length), np.float32)
    for line in range(2):
        for slot in (0, half):
            zed[line, :, line, slot] = cosm[:, slot]
        slots = slice(line * half + 1, (line + 1) * half)
        zed[line, :, 0, slots] = cosm[:, 1:half]
        zed[line, :, 1, slots] = -sinm[:, 1:half].astype(np.float32)
    dez = 2.0 * zed
    dez[:, :, :, 0] *= 0.5
    dez[:, :, :, half] *= 0.5
    zed = zed.reshape(2 * length, 2 * length).astype(ahead.dtype)
    dez = dez.reshape(2 * length, 2 * length).T.astype(ahead.dtype)
    return (ahead[order], zed), (ahead, back, back[:, order], dez)


def mirror_tables(length):
    half = length // 2
    index = np.arange(length)
    frequency = np.where(index <= half, index, index - half)
    wanted = -frequency % length
    whole = index[:, None] == wanted[None, :]
    low = (index[:, None] < half) & (index[:, None] + half == wanted[None, :])
    high = (index[:, None] >= half) & whole
    flip = index[:, None] == (-index % length)[None, :]
    return np.stack([flip, low, high, whole]).astype(np.float32).astype(jnp.bfloat16)


def dot(left, right):
    return jnp.dot(left, right, preferred_element_type=F32)


def planes_forward(own_ref, other_ref, table_ref, out_ref, held, sems):
    planes, length = own_ref.shape[0], own_ref.shape[1]
    groups = out_ref.shape[0]
    copies = []
    for x in range(0, planes, 2):
        own = own_ref[x : x + 2].astype(F32).reshape(2 * length, length)
        other = other_ref[x : x + 2].astype(F32).reshape(2 * length, length)
        field = jnp.concatenate([(own * own).astype(BF16), (own * other).astype(BF16)], axis=1)
        field = dot(field, table_ref[ZED]).astype(BF16)
        field = jnp.concatenate(
            [
                jnp.concatenate([field[:length, :length], field[length:, :length]], axis=1),
                jnp.concatenate([field[:length, length:], field[length:, length:]], axis=1),
            ],
            axis=0,
        )
        field = dot(table_ref[AHEAD_SORTED], field).astype(BF16)
        held[:, x] = field[:, :length].reshape(groups, -1, length)
        held[:, x + 1] = field[:, length:].reshape(groups, -1, length)
        copies.append(
            pltpu.make_async_copy(held.at[:, x : x + 2], out_ref.at[:, x : x + 2], sems.at[x // 2])
        )
        copies[-1].start()
    for copy in copies:
        copy.wait()


def columns_filter(line_ref, screen_ref, table_ref, out_ref, sent):
    length = line_ref.shape[0]
    columns = line_ref.shape[1] // 2
    lines = jnp.swapaxes(line_ref[...], 0, 1)
    for c in range(0, columns, 2):
        rows = [[part * columns + c + j for j in range(2)] for part in range(2)]
        field = jnp.concatenate(
            [jnp.concatenate([lines[row] for row in pair], axis=1) for pair in rows], axis=0
        )
        field = dot(table_ref[AHEAD], field)
        screen = jnp.concatenate([screen_ref[c], screen_ref[c + 1]], axis=1)
        field = jnp.concatenate([field[:length] * screen, field[length:] * screen], axis=0)
        field = dot(table_ref[BACK], field.astype(BF16)).astype(BF16)
        for part in range(2):
            for j in range(2):
                sent[rows[part][j]] = field[
                    part * length : (part + 1) * length, j * length : (j + 1) * length
                ]
    out_ref[...] = jnp.swapaxes(sent[...], 0, 1)


def back_along_y(line_ref, table_ref, x):
    length = line_ref.shape[3]
    field = jnp.concatenate(
        [line_ref[:, x + j].reshape(2 * length, length) for j in range(2)], axis=1
    )
    field = dot(table_ref[BACK_SORTED], field).astype(BF16)
    return jnp.concatenate(
        [
            jnp.concatenate([field[:length, :length], field[length:, :length]], axis=1),
            jnp.concatenate([field[:length, length:], field[length:, length:]], axis=1),
        ],
        axis=0,
    )


def planes_sent(line_ref, own_ref, table_ref, sent_ref):
    planes, length = own_ref.shape[0], own_ref.shape[1]
    for x in range(0, planes, 2):
        field = back_along_y(line_ref, table_ref, x)
        field = dot(field, table_ref[DEZ])[:, length:]
        own = own_ref[x : x + 2].astype(F32).reshape(2 * length, length)
        sent_ref[x : x + 2] = (field * own).astype(BF16).reshape(2, length, length)


def planes_kept(line_ref, own_ref, other_ref, table_ref, kept_ref):
    planes, length = own_ref.shape[0], own_ref.shape[1]
    for x in range(0, planes, 2):
        field = dot(back_along_y(line_ref, table_ref, x), table_ref[DEZ])
        own = own_ref[x : x + 2].astype(F32).reshape(2 * length, length)
        other = other_ref[x : x + 2].astype(F32).reshape(2 * length, length)
        kept = field[:, :length] * own + field[:, length:] * other
        kept_ref[x : x + 2] = kept.reshape(2, length, length)


def relay(there_ref, out_ref):
    out_ref[...] = there_ref[...]


def symmetric_kernel(here_ref, first_ref, second_ref, mirror_ref, out_ref, low, high, zero):
    columns, length = out_ref.shape[0], out_ref.shape[1]
    half = length // 2
    packed = half * columns
    odd = lax.rem(lax.axis_index("band"), 2)

    def spread(main_ref, edge_ref):
        row = lax.broadcasted_iota(jnp.int32, (packed, length), 0)
        main, edge = main_ref[:packed].astype(F32), edge_ref[:packed].astype(F32)
        block = jnp.where(lax.rem(row, columns) == 0, edge, main).astype(BF16)
        for out, choice in ((low, LOW), (high, HIGH)):
            out[...] = dot(block, mirror_ref[choice])
        row = lax.broadcasted_iota(jnp.int32, (SPARE, length), 0)
        main, edge = main_ref[packed:].astype(F32), edge_ref[packed:].astype(F32)
        zero[...] = jnp.where(row == 0, edge, main)

    pl.when(odd == 0)(lambda: spread(first_ref, second_ref))
    pl.when(odd == 1)(lambda: spread(second_ref, first_ref))
    zeros = zero[...].astype(BF16)
    slot = lax.broadcasted_iota(jnp.int32, (length, length), 1)
    row = lax.broadcasted_iota(jnp.int32, (SPARE, length), 0)
    first = lax.broadcasted_iota(jnp.int32, (SPARE, length), 1) == 0
    for c in range(columns):
        source = (columns - c) % columns
        other = jnp.concatenate(
            [part[pl.ds(source, half, stride=columns), :] for part in (low, high)], axis=0
        )
        chosen = ((row == source) & first).astype(F32).astype(BF16)
        other = other + lax.dot_general(
            zeros, chosen, (((0,), (0,)), ((), ())), preferred_element_type=F32
        )
        other = dot(mirror_ref[FLIP], other.astype(BF16))
        here = here_ref[pl.ds(c, length, stride=columns), :]
        here = jnp.where(slot <= half, here, pltpu.roll(here, half, 1))
        out_ref[c] = 0.5 * (here + other)


def prepare(first, own_ref, kernel_ref, table_ref, *refs):
    own_out, kernel_out, table_out, packed_out, sems = refs[-5:]

    band = lax.axis_index("band")
    early = (lax.rem(band, 2) == 1) & (band < lax.axis_size("band") - 1)

    if not first:

        @pl.when(early)
        def _():
            for made, out in zip(refs[:4], refs[4:8]):
                out[...] = made[...]

    @pl.when(early == first)
    def _():
        pairs = (
            (kernel_ref, kernel_out),
            (own_ref, own_out),
            (table_ref, table_out),
        )
        copies = [pltpu.make_async_copy(a, b, sems.at[i]) for i, (a, b) in enumerate(pairs)]
        for copy in copies:
            copy.start()
        copies[0].wait()
        length = kernel_out.shape[1]
        half = length // 2
        columns = kernel_out.shape[0] // length
        packed = half * columns
        lane = lax.broadcasted_iota(jnp.int32, (packed, length), 1)
        packed_out[:packed] = jnp.where(
            lane < half, pltpu.roll(kernel_out[:packed], half, 1), kernel_out[packed:]
        ).astype(BF16)
        row = lax.broadcasted_iota(jnp.int32, (SPARE, length), 0)
        first = lax.broadcasted_iota(jnp.int32, (SPARE, length), 1) == 0
        zeros = jnp.zeros((SPARE, length), F32)
        for c in range(columns):
            plane = kernel_out[pl.ds(c, length, stride=columns), :].astype(BF16)
            chosen = ((row == c) & first).astype(F32).astype(BF16)
            zeros = zeros + lax.dot_general(
                chosen, plane, (((1,), (1,)), ((), ())), preferred_element_type=F32
            )
        packed_out[packed:] = zeros.astype(BF16)
        for copy in copies[1:]:
            copy.wait()


def load(later_ref, table_ref, mirror_ref, table_out, mirror_out, sems):
    pairs = ((table_ref, table_out), (mirror_ref, mirror_out))
    copies = [pltpu.make_async_copy(a, b, sems.at[i]) for i, (a, b) in enumerate(pairs)]
    for copy in copies:
        copy.start()
    for copy in copies:
        copy.wait()


def finish(kept_ref, returned_ref, out_ref, held, sems):
    copies = []
    for i in range(sems.shape[0]):
        part = pl.ds(i * (held.shape[0] // sems.shape[0]), held.shape[0] // sems.shape[0])
        held[part] = kept_ref[part] + returned_ref[part].astype(F32)
        copies.append(pltpu.make_async_copy(held.at[part], out_ref.at[part], sems.at[i]))
        copies[-1].start()
    for copy in copies:
        copy.wait()


def call(body, outs, scratch=(), flops=0, name=None, in_specs=None, out_specs=None, aliases=None,
         limit=VMEM_LIMIT):
    specs = {"in_specs": in_specs, "out_specs": out_specs}
    specs = {key: value for key, value in specs.items() if value is not None}
    return pl.pallas_call(
        body,
        **specs,
        out_shape=outs,
        scratch_shapes=list(scratch),
        input_output_aliases=aliases or {},
        cost_estimate=pl.CostEstimate(flops=flops, bytes_accessed=1 << 20, transcendentals=0),
        compiler_params=pltpu.CompilerParams(vmem_limit_bytes=limit),
        name=name,
    )


def per_device(orbitals, kernel):
    planes, length = orbitals.shape[1], orbitals.shape[2]
    groups = lax.axis_size("fft")
    columns = length // groups
    near, far = (jnp.asarray(np.stack(some)) for some in complex_tables(length, groups))
    mirrors = jnp.asarray(mirror_tables(length))
    work = 8 * planes * length**3

    here = jax.ShapeDtypeStruct((length * columns, length), F32)
    sources = [
        pltpu.with_memory_space_constraint(array, pltpu.HBM)
        for array in (orbitals[0], kernel.reshape(here.shape), near, far, mirrors)
    ]
    results = (
        pltpu.VMEM(orbitals.shape[1:], BF16),
        pltpu.VMEM(here.shape, F32),
        pltpu.VMEM(near.shape, BF16),
        pltpu.VMEM((length // 2 * columns + SPARE, length), BF16),
    )
    anywhere = pl.BlockSpec(memory_space=pl.ANY)
    in_vmem = pl.BlockSpec(memory_space=pltpu.VMEM)
    prepared = call(
        functools.partial(prepare, True),
        results,
        [pltpu.SemaphoreType.DMA((3,))],
        in_specs=[anywhere] * 3,
        limit=NEARLY_ALL,
        name="prepare",
    )(*sources[:3])
    orbitals, *prepared = lax.optimization_barrier((orbitals, *prepared))
    other = from_behind(orbitals[0], "band", 1)
    own, here, near, packed = call(
        functools.partial(prepare, False),
        results,
        [pltpu.SemaphoreType.DMA((3,))],
        in_specs=[anywhere] * 3 + [in_vmem] * 4,
        aliases={3 + i: i for i in range(4)},
        name="prepare",
    )(*sources[:3], *prepared)
    bands = lax.axis_size("band")
    swap = [
        (b * groups + f, b * groups + (groups - 1 - f if b % 2 == 0 else -f % groups))
        for b in range(bands)
        for f in range(groups)
    ]
    there = lax.ppermute(packed, ("band", "fft"), swap)
    relayed = call(
        relay,
        jax.ShapeDtypeStruct(there.shape, BF16),
        flops=100 * 10**9,
        name="relay",
    )(there)
    swapped = from_behind(relayed, "band", -1)
    far, mirrors = call(
        load,
        (jax.ShapeDtypeStruct(far.shape, BF16), jax.ShapeDtypeStruct(mirrors.shape, BF16)),
        [pltpu.SemaphoreType.DMA((2,))],
        in_specs=[anywhere] * 3,
        name="load",
    )(relayed, *sources[3:])

    lines = jax.ShapeDtypeStruct((groups, planes, 2 * columns, length), BF16)
    spectrum = call(
        planes_forward,
        pltpu.HBM(lines.shape, lines.dtype),
        [pltpu.VMEM(lines.shape, BF16), pltpu.SemaphoreType.DMA((planes // 2,))],
        out_specs=pl.BlockSpec(memory_space=pl.ANY),
        name="planes_forward",
    )(
        own, other, near
    )
    spectrum = lax.all_to_all(spectrum, "fft", split_axis=0, concat_axis=0, tiled=True)
    screen = call(
        symmetric_kernel,
        jax.ShapeDtypeStruct((columns, length, length), F32),
        [pltpu.VMEM((length // 2 * columns, length), F32)] * 2
        + [pltpu.VMEM((SPARE, length), F32)],
        flops=work,
        name="symmetric_kernel",
    )(
        here, relayed, swapped, mirrors
    )
    spectrum = call(
        columns_filter,
        jax.ShapeDtypeStruct((length, 2 * columns, length), BF16),
        [pltpu.VMEM((2 * columns, length, length), BF16)],
        flops=2 * work,
        name="columns_filter",
    )(
        spectrum.reshape(length, 2 * columns, length),
        screen,
        far,
    )
    spectrum = spectrum.reshape(groups, planes, 2 * columns, length)
    spectrum = lax.all_to_all(spectrum, "fft", split_axis=0, concat_axis=0, tiled=True)
    sent = call(
        planes_sent,
        jax.ShapeDtypeStruct(own.shape, BF16),
        flops=work,
        name="planes_sent",
    )(spectrum, own, far)
    returned = from_behind(sent, "band", -1)
    kept = call(
        planes_kept,
        jax.ShapeDtypeStruct(own.shape, F32),
        flops=2 * work,
        name="planes_kept",
    )(spectrum, own, other, far)
    total = call(
        finish,
        jax.ShapeDtypeStruct(kept.shape, F32),
        [pltpu.VMEM(kept.shape, F32), pltpu.SemaphoreType.DMA((4,))],
        out_specs=pl.BlockSpec(memory_space=pl.ANY),
        name="finish",
    )(kept, returned)
    return total[None]


def solution(mesh):
    in_specs = (P("band", "fft", None, None), P(None, "fft", None))
    out_specs = P("band", "fft", None, None)
    return jax.shard_map(
        per_device, mesh=mesh, in_specs=in_specs, out_specs=out_specs, check_vma=False
    )
```
